512 devices in a mesh: ta: 32 (over z_hi, x, core), ha: 2 (over z_lo), wa: 8 (over y).
Axes of the slice: x: 4, y: 8, z: 8 (z_hi: 4, z_lo: 2; z = z_hi * 2 + z_lo), core: 2. Of those that a mesh axis runs over, the one named last changes fastest.
Arguments:
- queries: bfloat16 [96, 8, 32, 2048], P('ta', 'ha', 'wa'), may hold values from -6 to 61
- keys: bfloat16 [96, 8, 32, 2048], P('ta', 'ha', 'wa'), may hold values from -6 to 61
- values: bfloat16 [96, 8, 32, 2048], P('ta', 'ha', 'wa'), may hold values from -6 to 6
- query_gain: float32 [128], replicated, may hold values from 0.5 to 5
- key_gain: float32 [128], replicated, may hold values from 0.5 to 5
Outputs:
- attended: bfloat16 [96, 8, 32, 2048], P('ta', 'ha', 'wa')
The draws below stay inside these ranges and needn't reach their ends.
All inputs are finite; a program needn't handle non-finite values.
Results may differ from the reference program's by a relative error of at most 0.0025.
The reference program's roundings to bfloat16 on the way count: a program that leaves them out, or rounds other values in their place, can miss the bound.
Values may be sent and summed in bfloat16 or wider, within the bound.
A program may use at most 64 MiB of HBM per device.

```python
import math
import jax
import jax.numpy as jnp
from jax import lax

HEADS = 16
HEAD_DIM = 128
TILE_T = 6
TILE_H = 8
TILE_W = 8
FRAMES = 96
ROWS = 8
COLS = 32
FEATURES = 2048


def draw_queries(key, part):
    key = jax.random.fold_in(key, 1)
    full_shape = (FRAMES, ROWS, COLS, HEADS, HEAD_DIM)
    base_draw = jnp.clip(jax.random.normal(key, full_shape, jnp.float32), -6.0, 6.0)
    return base_draw.reshape(FRAMES, ROWS, COLS, HEADS * HEAD_DIM).astype(jnp.bfloat16)


def draw_keys(key, part):
    key = jax.random.fold_in(key, 2)
    full_shape = (FRAMES, ROWS, COLS, HEADS, HEAD_DIM)
    base_draw = jnp.clip(jax.random.normal(key, full_shape, jnp.float32), -6.0, 6.0)
    return base_draw.reshape(FRAMES, ROWS, COLS, HEADS * HEAD_DIM).astype(jnp.bfloat16)


def draw_query_gain(key, part):
    key = jax.random.fold_in(key, 3)
    gain_draw = jnp.exp(jax.random.uniform(key, (HEAD_DIM,), jnp.float32, -0.693, 0.693))
    return gain_draw


def draw_key_gain(key, part):
    key = jax.random.fold_in(key, 4)
    gain_draw = jnp.exp(jax.random.uniform(key, (HEAD_DIM,), jnp.float32, -0.693, 0.693))
    return gain_draw


def shard_levels(rng, extent, shards, least, largest):
    gain = 1.0
    for position, shards_of in shards:
        steps = jax.random.uniform(jax.random.fold_in(jax.random.fold_in(rng, 6), position), (shards_of,), jnp.float32, least / len(shards), largest / len(shards))
        gain = gain * jnp.repeat(jnp.exp(steps), extent[position] // shards_of).reshape((-1,) + (1,) * (len(extent) - 1 - position))
    return gain


def scatter_about(key, shape, deviation, limit, cuts=(), kind=jnp.bfloat16):
    values = jax.random.normal(key, shape, jnp.float32) * deviation
    if len(cuts) > 0:
        values = shard_levels(key, shape, cuts, -0.22, 0.18) * values
    return jnp.clip(values, min=-limit, max=limit).astype(kind)


def setup_inputs(seed: int = 0) -> dict:
    key_of = jax.random.split(jax.random.key(seed), 6)
    return {
        "queries": draw_queries(jax.random.fold_in(key_of[5], 71), 0),
        "keys": draw_keys(jax.random.fold_in(key_of[5], 71), 0),
        "values": scatter_about(key_of[2], (FRAMES, ROWS, COLS, FEATURES), 1.0, 6.0, ((0, 32), (1, 2), (2, 8))),
        "query_gain": draw_query_gain(jax.random.fold_in(key_of[5], 71), 0),
        "key_gain": draw_key_gain(jax.random.fold_in(key_of[5], 71), 0),
    }


epsilon = 1e-06

def normalize(tensor, gain_vec):
    head_dim = gain_vec.shape[0]
    per_head = tensor.astype(jnp.float32).reshape(tensor.shape[:-1] + (tensor.shape[-1] // head_dim, head_dim))
    mean_sq = lax.optimization_barrier(jnp.mean(per_head * per_head, axis=-1, keepdims=True))
    scaled = per_head * lax.rsqrt(mean_sq + epsilon) * gain_vec.astype(jnp.float32)
    return scaled.reshape(tensor.shape).astype(jnp.bfloat16)

def reference(queries, keys, values, query_gain, key_gain):
    frames, row_count, col_count, feature_width = queries.shape
    head_dim = query_gain.shape[0]
    head_count = feature_width // head_dim
    frame_tiles = frames // TILE_T
    row_tiles = row_count // TILE_H
    col_tiles = col_count // TILE_W
    row_window_span = min(3, row_tiles)
    col_win = min(3, col_tiles)
    tile_len = TILE_T * TILE_H * TILE_W
    score_scale = 1.0 / math.sqrt(head_dim)
    zero_index = jnp.zeros((), jnp.int32)

    def one_head(head_index):
        head_start = (head_index * head_dim).astype(jnp.int32)
        q_head = normalize(lax.dynamic_slice_in_dim(queries, head_start, head_dim, 3), query_gain)
        k_head = normalize(lax.dynamic_slice_in_dim(keys, head_start, head_dim, 3), key_gain)
        v_head = lax.dynamic_slice_in_dim(values, head_start, head_dim, 3)
        stacked = jnp.stack((k_head, v_head), axis=3)
        stacked = jnp.pad(stacked, ((TILE_T, TILE_T), (0, 0), (0, 0), (0, 0), (0, 0)))

        def one_frame(tile_frame):
            frame_index = tile_frame - 1 + jnp.arange(3, dtype=jnp.int32)
            frame_good = (frame_index >= 0) & (frame_index < frame_tiles)

            def one_tile(item):
                tile_row = (item // col_tiles).astype(jnp.int32)
                tile_col = (item % col_tiles).astype(jnp.int32)
                q_anchor = ((tile_frame * TILE_T).astype(jnp.int32), (tile_row * TILE_H).astype(jnp.int32), (tile_col * TILE_W).astype(jnp.int32), zero_index)
                q_tile = lax.dynamic_slice(q_head, q_anchor, (TILE_T, TILE_H, TILE_W, head_dim)).reshape(tile_len, head_dim)
                row_first = jnp.clip(tile_row - 1, 0, row_tiles - row_window_span).astype(jnp.int32)
                col_first = jnp.clip(tile_col - 1, 0, col_tiles - col_win).astype(jnp.int32)
                k_anchor = ((tile_frame * TILE_T).astype(jnp.int32), (row_first * TILE_H).astype(jnp.int32), (col_first * TILE_W).astype(jnp.int32), zero_index, zero_index)
                nearby = lax.dynamic_slice(stacked, k_anchor, (3 * TILE_T, row_window_span * TILE_H, col_win * TILE_W, 2, head_dim))
                key_tile = nearby[:, :, :, 0, :].reshape(-1, head_dim)
                value_tile = nearby[:, :, :, 1, :].reshape(-1, head_dim)
                row_good = jnp.abs(row_first + jnp.arange(row_window_span, dtype=jnp.int32) - tile_row) <= 1
                col_good = jnp.abs(col_first + jnp.arange(col_win, dtype=jnp.int32) - tile_col) <= 1
                key_ok = frame_good[:, None, None, None, None, None] & row_good[None, None, :, None, None, None] & col_good[None, None, None, None, :, None]
                key_ok = jnp.broadcast_to(key_ok, (3, TILE_T, row_window_span, TILE_H, col_win, TILE_W)).reshape(-1)
                scores = jnp.einsum('qd,kd->qk', q_tile.astype(jnp.float32), key_tile.astype(jnp.float32)) * score_scale
                scores = jnp.where(key_ok[None, :], scores, -jnp.inf)
                row_max = lax.optimization_barrier(jnp.max(scores, axis=1, keepdims=True))
                weights = jnp.exp(scores - row_max)
                row_total = lax.optimization_barrier(jnp.sum(weights, axis=1, keepdims=True))
                rounded = lax.optimization_barrier(weights.astype(jnp.bfloat16))
                summed = jnp.einsum('qk,kd->qd', rounded.astype(jnp.float32), value_tile.astype(jnp.float32))
                return (summed / row_total).astype(jnp.bfloat16)
            tiles = jax.vmap(one_tile)(jnp.arange(row_tiles * col_tiles, dtype=jnp.int32))
            tiles = tiles.reshape(row_tiles, col_tiles, TILE_T, TILE_H, TILE_W, head_dim)
            return tiles.transpose(2, 0, 3, 1, 4, 5).reshape(TILE_T, row_count, col_count, head_dim)
        out_frames = lax.map(one_frame, jnp.arange(frame_tiles, dtype=jnp.int32))
        return out_frames.reshape(frames, row_count, col_count, head_dim)
    result = lax.map(one_head, jnp.arange(head_count, dtype=jnp.int32))
    return jnp.moveaxis(result, 0, 3).reshape(frames, row_count, col_count, feature_width)
```

```python
import functools
import math

import jax
import jax.numpy as jnp
from jax import lax
from jax.experimental import pallas as pl
from jax.experimental.pallas import tpu as pltpu
from jax.sharding import PartitionSpec as P

MESH = pl.DeviceIdType.MESH
EPSILON = 1e-06
HEADS = 16
DIM = 128
TOKENS = 48
SOURCES = 8
TILE = SOURCES * TOKENS
HALF = TILE // 2
SCORE_SCALE = 1.0 / math.sqrt(DIM)
EXP2_SCALE = SCORE_SCALE * math.log2(math.e)


def normed(x, gain):
    mean_sq = jnp.mean(x * x, axis=-1, keepdims=True)
    return x * lax.rsqrt(mean_sq + EPSILON) * gain


def kernel(
    q_ref, k_ref, v_ref, qg_ref, kg_ref, o_ref,
    qs, ks, vs, qb, kb, vb, osend, ob, s_narrow, s_wide, m_ref, l_ref, acc_ref,
    own_send, own_self, q_recv, k_recv, v_recv, k_edge, v_edge, k_near, v_near,
    fwd_send, out_send, out_recv,
):
    ta, zl, y = lax.axis_index("ta"), lax.axis_index("ha"), lax.axis_index("wa")
    frame, core = ta // 2, lax.rem(ta, 2)
    last_frame = lax.axis_size("ta") // 2 - 1
    chip = y * 2 + zl
    to_core = y // 4
    own = core == to_core
    has_low, has_high = frame > 0, frame < last_frame

    def device(f, c, z, w):
        return {"ta": f * 2 + c, "ha": z, "wa": w}

    barrier = pltpu.get_barrier_semaphore()

    def greet(f, c, z, w):
        pl.semaphore_signal(barrier, inc=1, device_id=device(f, c, z, w), device_id_type=MESH)

    def greet_step(n, carry):
        @pl.when(jnp.logical_or(n != chip, jnp.logical_not(own)))
        def _():
            greet(frame, to_core, lax.rem(n, 2), n // 2)

        z, c, w = lax.rem(n // 2, 2), lax.rem(n, 2), core * 4 + n // 4
        @pl.when(jnp.logical_or(z * 1 + w * 2 != chip, c != core))
        def _():
            greet(frame, c, z, w)

        return carry

    lax.fori_loop(0, HEADS, greet_step, 0)
    greet(frame, 1 - core, zl, y)

    @pl.when(has_low)
    def _():
        greet(frame - 1, 0, zl, y)
        greet(frame - 1, 1, zl, y)

    @pl.when(has_high)
    def _():
        greet(frame + 1, 0, zl, y)
        greet(frame + 1, 1, zl, y)

    for n in range(HEADS):
        lanes = slice(n * DIM, (n + 1) * DIM)
        k = k_ref[:, :, :, lanes].astype(jnp.float32).reshape(TOKENS, DIM)
        ks[n] = normed(k, kg_ref[...]).astype(jnp.bfloat16)
    for n in range(HEADS):
        lanes = slice(n * DIM, (n + 1) * DIM)
        q = q_ref[:, :, :, lanes].astype(jnp.float32).reshape(TOKENS, DIM)
        qs[n] = normed(q, qg_ref[...]).astype(jnp.bfloat16)
        v = v_ref[:, :, :, lanes].astype(jnp.float32).reshape(TOKENS, DIM)
        vs[n] = v.astype(jnp.bfloat16)

    greetings = (
        1 + 2 * HEADS
        - jnp.where(own, 2, 0)
        + jnp.where(has_low, 2, 0)
        + jnp.where(has_high, 2, 0)
    )
    pl.semaphore_wait(barrier, greetings)

    col = y // 2
    tile = lax.rem(col, 2)
    rows = pl.ds((lax.rem(y, 2) * 4 + zl * 2 + core) * TOKENS, TOKENS)
    k_to = kb.at[1, col - to_core, rows]
    v_to = vb.at[1, col - to_core, rows]
    q_to = qb.at[tile, rows]
    group = tile * 2 + lax.rem(y, 2)

    def block_send(which, source, target, recv, n):
        return pltpu.make_async_remote_copy(
            src_ref=source.at[n], dst_ref=target,
            send_sem=own_send.at[which], recv_sem=recv,
            device_id=device(frame, to_core, lax.rem(n, 2), n // 2), device_id_type=MESH,
        )

    blocks = (
        (0, ks, k_to, k_recv.at[group]),
        (1, qs, q_to, q_recv.at[tile]),
        (2, vs, v_to, v_recv.at[group]),
    )

    def block_self(which, source, target, recv):
        return (
            pltpu.make_async_copy(source.at[chip], target, recv),
            pltpu.make_async_remote_copy(
                src_ref=source.at[chip], dst_ref=target,
                send_sem=own_self.at[which], recv_sem=recv,
                device_id=device(frame, 1 - core, zl, y), device_id_type=MESH,
            ),
        )

    for which, source, target, recv in blocks:
        here, there = block_self(which, source, target, recv)

        @pl.when(own)
        def _(here=here):
            here.start()

        @pl.when(jnp.logical_not(own))
        def _(there=there):
            there.start()

        def send_step(j, carry, which=which, source=source, target=target, recv=recv):
            turn = j // 2
            offset = (turn + 1) // 2 * (2 * lax.rem(turn, 2) - 1)
            to_y = lax.rem(y + offset + 8, 8)
            to_z = lax.rem(zl + j, 2)
            block_send(which, source, target, recv, to_y * 2 + to_z).start()
            return carry

        lax.fori_loop(1, HEADS, send_step, 0)

    def forwards(kind, buf, edge, near, step):
        at_edge = step < 2
        t = 1 - core if at_edge else core
        part = pl.ds(step % 2 * HALF, HALF)
        source = buf.at[1, core + t, part]
        copies = []

        def add(cond, target, recv, f, c, i):
            copies.append((cond, pltpu.make_async_remote_copy(
                src_ref=source, dst_ref=target,
                send_sem=fwd_send.at[kind, step, i], recv_sem=recv,
                device_id=device(f, c, zl, y), device_id_type=MESH,
            )))

        add(has_high, buf.at[0, core + t, part], near.at[0], frame + 1, core, 0)
        add(has_low, buf.at[2, core + t, part], near.at[1], frame - 1, core, 1)
        if at_edge:
            slot = 2 * core
            add(None, buf.at[1, slot, part], edge, frame, 1 - core, 2)
            add(has_high, buf.at[0, slot, part], near.at[0], frame + 1, 1 - core, 3)
            add(has_low, buf.at[2, slot, part], near.at[1], frame - 1, 1 - core, 4)
        return copies

    def each(copies, act):
        for cond, copy in copies:
            if cond is None:
                act(copy)
            else:
                @pl.when(cond)
                def _(copy=copy):
                    act(copy)

    def landed(ref, sem):
        pltpu.make_async_copy(ref, ref, sem).wait()

    def pass_on(kind, buf, recv, edge, near):
        for step in range(4):
            t = 1 - core if step < 2 else core
            part = pl.ds(step % 2 * HALF, HALF)
            landed(buf.at[1, core + t, part], recv.at[t * 2 + step % 2])
            each(forwards(kind, buf, edge, near, step), lambda copy: copy.start())

    def score(which, p):
        count = 2 + which
        t, scores = ((core, s_narrow), (1 - core, s_wide))[which]
        first = core if which == 0 else 0
        q = qb[t]
        k = kb[p, pl.ds(first, count)].reshape(count * TILE, DIM)
        s = lax.dot_general(q, k, (((1,), (1,)), ((), ())), preferred_element_type=jnp.float32)
        scores[p] = s
        best = s[:, :DIM] if p == 1 else m_ref[which]
        for c in range(1 if p == 1 else 0, count * TILE // DIM):
            best = jnp.maximum(best, s[:, c * DIM : (c + 1) * DIM])
        m_ref[which] = best

    def weigh(which, p):
        count = 2 + which
        scores = (s_narrow, s_wide)[which]
        first = core if which == 0 else 0
        s = scores[p]
        best = m_ref[which][:, :1]
        w = jnp.exp2((s - best) * EXP2_SCALE)
        total = w[:, :DIM]
        for c in range(1, count * TILE // DIM):
            total = total + w[:, c * DIM : (c + 1) * DIM]
        v = vb[p, pl.ds(first, count)].reshape(count * TILE, DIM)
        part = lax.dot_general(
            w.astype(jnp.bfloat16), v, (((1,), (0,)), ((), ())), preferred_element_type=jnp.float32
        )
        if p == 1:
            l_ref[which] = total
            acc_ref[which] = part
        else:
            l_ref[which] += total
            acc_ref[which] += part

    def sides(act):
        @pl.when(has_low)
        def _():
            act(0, 0)

        @pl.when(has_high)
        def _():
            act(2, 1)

    pass_on(0, kb, k_recv, k_edge, k_near)
    landed(qb.at[0], q_recv.at[0])
    landed(qb.at[1], q_recv.at[1])
    score(0, 1)
    pass_on(1, vb, v_recv, v_edge, v_near)
    landed(kb.at[1, 2 - 2 * core], k_edge)
    score(1, 1)

    def score_side(p, i):
        landed(kb.at[p], k_near.at[i])
        score(0, p)
        score(1, p)

    sides(score_side)
    for which in range(2):
        m_ref[which] = jnp.broadcast_to(
            jnp.max(m_ref[which], axis=1, keepdims=True), (TILE, DIM)
        )
    weigh(0, 1)
    landed(vb.at[1, 2 - 2 * core], v_edge)
    weigh(1, 1)

    def weigh_side(p, i):
        landed(vb.at[p], v_near.at[i])
        weigh(0, p)

    sides(weigh_side)

    def out_copy(which, i):
        t = (core, 1 - core)[which]
        w, z, c = core * 4 + t * 2 + i // 4, lax.rem(i // 2, 2), lax.rem(i, 2)
        part = osend.at[which, pl.ds(i * TOKENS, TOKENS)]
        here = jnp.logical_and(w * 2 + z == chip, c == core)
        return here, pltpu.make_async_copy(part, ob.at[chip], out_recv), pltpu.make_async_remote_copy(
            src_ref=part, dst_ref=ob.at[chip], send_sem=out_send.at[which, i], recv_sem=out_recv,
            device_id=device(frame, c, z, w), device_id_type=MESH,
        )

    def finish(which):
        total = jnp.sum(l_ref[which], axis=1, keepdims=True)
        osend[which] = (acc_ref[which] / total).astype(jnp.bfloat16)

        def step(i, carry):
            here, local, remote = out_copy(which, i)

            @pl.when(here)
            def _():
                local.start()

            @pl.when(jnp.logical_not(here))
            def _():
                remote.start()

            return carry

        lax.fori_loop(0, SOURCES, step, 0)

    finish(0)
    sides(lambda p, i: weigh(1, p))
    finish(1)

    landed(ob, out_recv)
    for n in range(HEADS):
        o = ob[n].astype(jnp.float32).reshape(3, 4, 4, DIM)
        o_ref[:, :, :, n * DIM : (n + 1) * DIM] = o.astype(jnp.bfloat16)

    for which, source, target, recv in blocks:
        many = source.at[pl.ds(0, HEADS - 1)]
        pltpu.make_async_copy(many, many, own_send.at[which]).wait()
        _, there = block_self(which, source, target, recv)

        @pl.when(jnp.logical_not(own))
        def _(there=there):
            there.wait_send()

    for step in range(4):
        each(forwards(0, kb, k_edge, k_near, step), lambda copy: copy.wait_send())
        each(forwards(1, vb, v_edge, v_near, step), lambda copy: copy.wait_send())

    def out_done(i, carry):
        for which in range(2):
            here, _, remote = out_copy(which, i)

            @pl.when(jnp.logical_not(here))
            def _(remote=remote):
                remote.wait_send()

        return carry

    lax.fori_loop(0, SOURCES, out_done, 0)


def per_device(queries, keys, values, query_gain, key_gain):
    bf16, f32 = jnp.bfloat16, jnp.float32
    dma, vmem = pltpu.SemaphoreType.DMA, pltpu.VMEM
    return pl.pallas_call(
        kernel,
        out_shape=jax.ShapeDtypeStruct(queries.shape, bf16),
        in_specs=[pl.BlockSpec(memory_space=pltpu.VMEM)] * 5,
        out_specs=pl.BlockSpec(memory_space=pltpu.VMEM),
        scratch_shapes=[
            vmem((HEADS, TOKENS, DIM), bf16),
            vmem((HEADS, TOKENS, DIM), bf16),
            vmem((HEADS, TOKENS, DIM), bf16),
            vmem((2, TILE, DIM), bf16),
            vmem((3, 3, TILE, DIM), bf16),
            vmem((3, 3, TILE, DIM), bf16),
            vmem((2, TILE, DIM), bf16),
            vmem((HEADS, TOKENS, DIM), bf16),
            vmem((3, TILE, 2 * TILE), f32),
            vmem((3, TILE, 3 * TILE), f32),
            vmem((2, TILE, DIM), f32),
            vmem((2, TILE, DIM), f32),
            vmem((2, TILE, DIM), f32),
            dma((3,)), dma((3,)), dma((2,)), dma((4,)), dma((4,)), dma, dma, dma((2,)), dma((2,)),
            dma((2, 4, 5)), dma((2, SOURCES)), dma,
        ],
        compiler_params=pltpu.CompilerParams(
            collective_id=0, has_side_effects=True, vmem_limit_bytes=48 * 1024 * 1024
        ),
        cost_estimate=pl.CostEstimate(
            flops=1100000000, bytes_accessed=800000, transcendentals=2200000
        ),
    )(queries, keys, values, query_gain.reshape(1, DIM), key_gain.reshape(1, DIM))


def solution(mesh):
    return jax.shard_map(
        per_device,
        mesh=mesh,
        in_specs=(
            P("ta", "ha", "wa", None),
            P("ta", "ha", "wa", None),
            P("ta", "ha", "wa", None),
            P(),
            P(),
        ),
        out_specs=P("ta", "ha", "wa", None),
        check_vma=False,
    )
```

```python
import math

import jax
import jax.numpy as jnp
from jax import lax
from jax.experimental import pallas as pl
from jax.experimental.pallas import tpu as pltpu
from jax.sharding import PartitionSpec as P

MESH = pl.DeviceIdType.MESH
EPSILON = 1e-06
HEADS = 16
DIM = 128
TOKENS = 48
SOURCES = 8
TILE = SOURCES * TOKENS
HALF = TILE // 2
LINE = 4
SCORE_SCALE = 1.0 / math.sqrt(DIM)

ROUTE = ((3, 3, 0, 0), (1, 2, 3, 0))

ARRIVALS = ((0, 1, 2, 3), (1, 0, 2, 3), (2, 1, 3, 0), (3, 2, 1, 0), (3, 2, 1, 0), (3, 2, 0, 1), (0, 3, 1, 2), (0, 1, 2, 3))
PACKED = tuple(sum(order[turn] * 4**place for place, order in enumerate(ARRIVALS)) for turn in range(4))
POWERS = tuple(4**place for place in range(8))


def normed(x, gain):
    mean_sq = jnp.mean(x * x, axis=-1, keepdims=True)
    return x * lax.rsqrt(mean_sq + EPSILON) * gain


def landed(ref, sem):
    pltpu.make_async_copy(ref, ref, sem).wait()


def kernel(
    q_hbm, k_hbm, v_hbm, qg_ref, kg_ref, o_ref,
    q_in, k_in, v_in, qs, ks, vs, qb, kb, vb, rb, osend, ob,
    s_narrow, s_wide, m_ref, l_ref, acc_ref,
    in_sem, own_send, own_self, q_recv, own_recv, edge_recv, near_recv, cross_recv, relay_recv,
    fwd_send, relay_send, cross_send, out_send, out_recv,
):
    ta, zl, y = lax.axis_index("ta"), lax.axis_index("ha"), lax.axis_index("wa")
    frame, core = ta // 2, lax.rem(ta, 2)
    other = 1 - core
    x = lax.rem(frame, LINE)
    last_frame = lax.axis_size("ta") // 2 - 1
    chip = y * 2 + zl
    to_core = y // 4
    own = core == to_core
    not_own = jnp.logical_not(own)
    has_low, has_high = frame > 0, frame < last_frame
    has = (has_low, has_high)
    first = frame - x
    turn_low = jnp.logical_and(x == 0, has_low)
    turn_high = jnp.logical_and(x == LINE - 1, has_high)
    relay_up = jnp.logical_and(x < LINE - 1, first + LINE <= last_frame)
    relay_down = jnp.logical_and(x > 0, first > 0)

    def device(f, c, z, w):
        return {"ta": f * 2 + c, "ha": z, "wa": w}

    copies_in = [
        pltpu.make_async_copy(src, dst, in_sem.at[i])
        for i, (src, dst) in enumerate(((k_hbm, k_in), (q_hbm, q_in), (v_hbm, v_in)))
    ]
    for copy in copies_in:
        copy.start()

    barrier = pltpu.get_barrier_semaphore()

    def greet(f, c, z, w):
        pl.semaphore_signal(barrier, inc=1, device_id=device(f, c, z, w), device_id_type=MESH)

    def greet_step(n, carry):
        z, c, w = lax.rem(n // 2, 2), lax.rem(n, 2), core * 4 + n // 4

        @pl.when(jnp.logical_or(w * 2 + z != chip, c != core))
        def _():
            greet(frame, c, z, w)

        return carry

    lax.fori_loop(0, HEADS, greet_step, 0)
    greet(frame, other, zl, y)
    for cond, f in (
        (has_low, frame - 1),
        (has_high, frame + 1),
        *((turn_low, frame - LINE + i) for i in range(LINE - 1)),
        *((turn_high, frame + LINE - i) for i in range(LINE - 1)),
        (relay_up, first + LINE - 1),
        (relay_down, first),
    ):
        @pl.when(cond)
        def _(f=f):
            greet(f, core, zl, y)

    def count(cond, amount=1):
        return jnp.where(cond, amount, 0)

    greetings = (
        1 + HEADS - count(own) + count(has_low) + count(has_high)
        + count(turn_low, LINE - 1) + count(turn_high, LINE - 1) + count(relay_up) + count(relay_down)
    )

    col = y // 2
    tile = lax.rem(col, 2)
    rows = pl.ds((lax.rem(y, 2) * 4 + zl * 2 + core) * TOKENS, TOKENS)
    group = lax.rem(y, 4)
    blocks = (
        (0, ks, kb.at[1, col - to_core, rows], own_recv.at[0, group]),
        (1, vs, vb.at[1, col - to_core, rows], own_recv.at[1, group]),
        (2, qs, qb.at[tile, rows], q_recv.at[tile]),
    )

    def block_self(which, source, target, recv):
        return (
            pltpu.make_async_copy(source.at[chip], target, recv),
            pltpu.make_async_remote_copy(
                src_ref=source.at[chip], dst_ref=target,
                send_sem=own_self.at[which], recv_sem=recv,
                device_id=device(frame, other, zl, y), device_id_type=MESH,
            ),
        )

    def send_blocks(which, source, target, recv):
        here, there = block_self(which, source, target, recv)

        @pl.when(own)
        def _():
            here.start()

        @pl.when(not_own)
        def _():
            there.start()

        def send_step(j, carry):
            turn = j // 2
            offset = (turn + 1) // 2 * (2 * lax.rem(turn, 2) - 1)
            to_y = lax.rem(y + offset + 8, 8)
            to_z = lax.rem(zl + j, 2)
            pltpu.make_async_remote_copy(
                src_ref=source.at[to_y * 2 + to_z], dst_ref=target,
                send_sem=own_send.at[which], recv_sem=recv,
                device_id=device(frame, to_core, to_z, to_y), device_id_type=MESH,
            ).start()
            return carry

        lax.fori_loop(1, HEADS, send_step, 0)

    def head(ref, n):
        return ref[:, :, :, n * DIM : (n + 1) * DIM].astype(jnp.float32).reshape(TOKENS, DIM)

    with jax.named_scope("norm_k"):
        copies_in[0].wait()
        for n in range(HEADS):
            ks[n] = normed(head(k_in, n), kg_ref[...]).astype(jnp.bfloat16)
    with jax.named_scope("barrier"):
        pl.semaphore_wait(barrier, greetings)
    with jax.named_scope("sends"):
        send_blocks(*blocks[0])
        copies_in[2].wait()
        for n in range(HEADS):
            vs[n] = head(v_in, n).astype(jnp.bfloat16)
        send_blocks(*blocks[1])
        copies_in[1].wait()
        for n in range(HEADS):
            qs[n] = normed(head(q_in, n), qg_ref[...]).astype(jnp.bfloat16)
        send_blocks(*blocks[2])

    place = lax.rem(y - 4 * core + 8, 8)
    power = jnp.int32(POWERS[0])
    for i in range(1, 8):
        power = jnp.where(place == i, POWERS[i], power)
    bufs = (kb, vb)

    def arriving(turn):
        g = lax.rem(PACKED[turn] // power, 4)
        return g, core + g // 2, pl.ds(lax.rem(g, 2) * HALF, HALF), g // 2 == other

    def forwards(kind, turn):
        buf = bufs[kind]
        g, slot, part, at_edge = arriving(turn)
        copies = []

        def add(i, cond, target, recv, f, c):
            copies.append((cond, pltpu.make_async_remote_copy(
                src_ref=buf.at[1, slot, part], dst_ref=target,
                send_sem=fwd_send.at[kind, turn, i], recv_sem=recv,
                device_id=device(f, c, zl, y), device_id_type=MESH,
            )))

        high = (1, buf.at[0, slot, part], near_recv.at[kind, 0, g], frame + 1, core)
        low = (0, buf.at[2, slot, part], near_recv.at[kind, 1, g], frame - 1, core)
        away = ROUTE[kind][turn]
        if away > 0:
            add(1, turn_high, rb.at[0, kind, turn], relay_recv.at[0, kind, turn], frame - away, core)
            add(0, turn_low, rb.at[1, kind, turn], relay_recv.at[1, kind, turn], frame + away, core)
            add(high[0], jnp.logical_and(has_high, x != LINE - 1), *high[1:])
            add(low[0], jnp.logical_and(has_low, x != 0), *low[1:])
        else:
            add(high[0], has_high, *high[1:])
            add(low[0], has_low, *low[1:])
        add(2, at_edge, buf.at[1, 2 * core, part], edge_recv.at[kind], frame, other)
        return copies

    def each(copies, act):
        for cond, copy in copies:
            @pl.when(cond)
            def _(copy=copy):
                act(copy)

    def pass_on(kind, turns):
        for turn in turns:
            g, slot, part, _ = arriving(turn)
            landed(bufs[kind].at[1, slot, part], own_recv.at[kind, g])
            each(forwards(kind, turn), lambda copy: copy.start())

    def relay_copy(way, kind, turn):
        g, slot, part, _ = arriving(turn)
        return pltpu.make_async_remote_copy(
            src_ref=rb.at[way, kind, turn], dst_ref=bufs[kind].at[2 * way, slot, part],
            send_sem=relay_send.at[way, kind, turn], recv_sem=near_recv.at[kind, way, g],
            device_id=device(first - 1 if way else first + LINE, core, zl, y), device_id_type=MESH,
        )

    def relays(kind, turns, act):
        for turn in turns:
            away = ROUTE[kind][turn]
            if away > 0:
                for way, cond in (
                    (0, jnp.logical_and(relay_up, x == LINE - 1 - away)),
                    (1, jnp.logical_and(relay_down, x == away)),
                ):
                    @pl.when(cond)
                    def _(way=way):
                        act(way, kind, turn)

    def relay(kind, turns):
        def pass_relay(way, kind, turn):
            landed(rb.at[way, kind, turn], relay_recv.at[way, kind, turn])
            relay_copy(way, kind, turn).start()

        relays(kind, turns, pass_relay)

    first_side = count(x == 0)

    def side(turn):
        i = first_side if turn == 0 else 1 - first_side
        return i, jnp.logical_or(jnp.logical_and(i == 0, has_low), jnp.logical_and(i == 1, has_high))

    def cross_copy(kind, i, turn):
        g, slot, part, at_edge = arriving(turn)
        return at_edge, pltpu.make_async_remote_copy(
            src_ref=bufs[kind].at[2 * i, slot, part], dst_ref=bufs[kind].at[2 * i, 2 * core, part],
            send_sem=cross_send.at[kind, i, g], recv_sem=cross_recv.at[kind, i],
            device_id=device(frame, other, zl, y), device_id_type=MESH,
        )

    def near(kind, i):
        for turn in range(4):
            g, slot, part, _ = arriving(turn)
            landed(bufs[kind].at[2 * i, slot, part], near_recv.at[kind, i, g])
            each([cross_copy(kind, i, turn)], lambda copy: copy.start())

    def crossed(kind, i):
        landed(bufs[kind].at[2 * i, 2 * other], cross_recv.at[kind, i])

    def sides(turn, act):
        i, cond = side(turn)

        @pl.when(cond)
        def _():
            act(i)

    def window(buf, which, p):
        start = core if which == 0 else 0
        return buf[p, pl.ds(start, 2 + which)].reshape((2 + which) * TILE, DIM)

    def score(which, p, fresh=False):
        t, scores = ((core, s_narrow), (other, s_wide))[which]
        s = lax.dot_general(
            qb[t], window(kb, which, p), (((1,), (1,)), ((), ())), preferred_element_type=jnp.float32
        ) * SCORE_SCALE
        scores[p] = s
        best = s[:, :DIM] if fresh else jnp.maximum(m_ref[which], s[:, :DIM])
        for c in range(1, (2 + which) * TILE // DIM):
            best = jnp.maximum(best, s[:, c * DIM : (c + 1) * DIM])
        m_ref[which] = best

    def attend(which, p, fresh=False, rows=slice(0, TILE)):
        scores = (s_narrow, s_wide)[which]
        start = core if which == 0 else 0
        best = m_ref[which, rows]
        total, acc = (None, None) if fresh else (l_ref[which, rows], acc_ref[which, rows])
        for c in range(2 + which):
            parts = []
            for d in range(TILE // DIM):
                lanes = slice(c * TILE + d * DIM, c * TILE + (d + 1) * DIM)
                w = jnp.exp(scores[p, rows, lanes] - best)
                total = w if total is None else total + w
                parts.append(w.astype(jnp.bfloat16))
            part = jnp.dot(
                jnp.concatenate(parts, axis=1), vb[p, start + c], preferred_element_type=jnp.float32
            )
            acc = part if acc is None else acc + part
        l_ref[which, rows] = total
        acc_ref[which, rows] = acc

    def out_copy(which, i):
        t = (core, other)[which]
        w, z, c = core * 4 + t * 2 + i // 4, lax.rem(i // 2, 2), lax.rem(i, 2)
        part = osend.at[which, pl.ds(i * TOKENS, TOKENS)]
        here = jnp.logical_and(w * 2 + z == chip, c == core)
        return here, pltpu.make_async_copy(part, ob.at[chip], out_recv), pltpu.make_async_remote_copy(
            src_ref=part, dst_ref=ob.at[chip], send_sem=out_send.at[which, i], recv_sem=out_recv,
            device_id=device(frame, c, z, w), device_id_type=MESH,
        )

    def finish(which, first_block=0, blocks_done=SOURCES):
        rows = slice(first_block * TOKENS, blocks_done * TOKENS)
        total = jnp.sum(l_ref[which, rows], axis=1, keepdims=True)
        osend[which, rows] = (acc_ref[which, rows] / total).astype(jnp.bfloat16)

        def step(i, carry):
            here, local, remote = out_copy(which, i)

            @pl.when(here)
            def _():
                local.start()

            @pl.when(jnp.logical_not(here))
            def _():
                remote.start()

            return carry

        lax.fori_loop(first_block, blocks_done, step, 0)

    for kind in range(2):
        for turn in range(4):
            with jax.named_scope(f"pass{kind}{turn}"):
                pass_on(kind, [turn])
            if kind == 1:
                with jax.named_scope(f"relay{turn}"):
                    relay(turn // 2, [turn % 2])
    with jax.named_scope("near_a"):
        sides(0, lambda i: near(0, i))
    with jax.named_scope("relay_last"):
        relay(1, [2])
    with jax.named_scope("wait_q"):
        landed(qb.at[0], q_recv.at[0])
        landed(qb.at[1], q_recv.at[1])
        landed(kb.at[1, 2 * other], edge_recv.at[0])
    with jax.named_scope("score"):
        score(0, 1, fresh=True)
        score(1, 1, fresh=True)

    def score_side(i):
        crossed(0, i)
        score(0, 2 * i)
        score(1, 2 * i)

    with jax.named_scope("score_a"):
        sides(0, score_side)
    with jax.named_scope("near_b"):
        sides(1, lambda i: near(0, i))
    with jax.named_scope("score_b"):
        sides(1, score_side)
    with jax.named_scope("attend"):
        landed(vb.at[1, 2 * other], edge_recv.at[1])
        for which in range(2):
            m_ref[which] = jnp.broadcast_to(jnp.max(m_ref[which], axis=1, keepdims=True), (TILE, DIM))
        attend(0, 1, fresh=True)
        attend(1, 1, fresh=True)
    with jax.named_scope("near_va"):
        sides(0, lambda i: near(1, i))

    turned = jnp.logical_or(turn_low, turn_high)
    straight = jnp.logical_not(turned)
    with jax.named_scope("near_vb1"):
        @pl.when(straight)
        def _():
            sides(1, lambda i: near(1, i))

    def attend_side(i):
        crossed(1, i)
        attend(0, 2 * i)

    with jax.named_scope("attend_0a"):
        sides(0, attend_side)

    with jax.named_scope("turned"):
        @pl.when(turned)
        def _():
            sides(0, lambda i: attend(1, 2 * i))
            sides(1, lambda i: near(1, i))

    with jax.named_scope("attend_0b"):
        sides(1, attend_side)
        finish(0)
    with jax.named_scope("attend_1a"):
        @pl.when(straight)
        def _():
            sides(0, lambda i: attend(1, 2 * i))

    with jax.named_scope("attend_1b"):
        for first_block in (0, SOURCES // 2):
            rows = slice(first_block * TOKENS, first_block * TOKENS + HALF)
            sides(1, lambda i: attend(1, 2 * i, rows=rows))
            finish(1, first_block, first_block + SOURCES // 2)

    with jax.named_scope("drain"):
        for which, source, target, recv in blocks:
            many = source.at[pl.ds(0, HEADS - 1)]
            landed(many, own_send.at[which])
            _, there = block_self(which, source, target, recv)

            @pl.when(not_own)
            def _(there=there):
                there.wait_send()

        for kind in range(2):
            for turn in range(4):
                each(forwards(kind, turn), lambda copy: copy.wait_send())
                for i in range(2):
                    at_edge, copy = cross_copy(kind, i, turn)

                    @pl.when(jnp.logical_and(at_edge, has[i]))
                    def _(copy=copy):
                        copy.wait_send()

            relays(kind, range(4), lambda way, kind, turn: relay_copy(way, kind, turn).wait_send())

    with jax.named_scope("wait_out"):
        landed(ob, out_recv)
    with jax.named_scope("write_out"):
        for n in range(HEADS):
            o = ob[n].astype(jnp.float32).reshape(3, 4, 4, DIM)
            o_ref[:, :, :, n * DIM : (n + 1) * DIM] = o.astype(jnp.bfloat16)

    with jax.named_scope("drain_out"):
        def out_done(i, carry):
            for which in range(2):
                here, _, remote = out_copy(which, i)

                @pl.when(jnp.logical_not(here))
                def _(remote=remote):
                    remote.wait_send()

            return carry

        lax.fori_loop(0, SOURCES, out_done, 0)


def per_device(queries, keys, values, query_gain, key_gain):
    bf16, f32 = jnp.bfloat16, jnp.float32
    dma, vmem = pltpu.SemaphoreType.DMA, pltpu.VMEM
    hbm = pl.BlockSpec(memory_space=pl.ANY)
    operands = (queries, keys, values, query_gain.reshape(1, DIM), key_gain.reshape(1, DIM))
    block = (HEADS, TOKENS, DIM)
    return pl.pallas_call(
        kernel,
        out_shape=jax.ShapeDtypeStruct(queries.shape, bf16),
        in_specs=[hbm] * 3 + [pl.BlockSpec(memory_space=pltpu.VMEM)] * 2,
        out_specs=pl.BlockSpec(memory_space=pltpu.VMEM),
        scratch_shapes=[
            vmem(queries.shape, bf16), vmem(queries.shape, bf16), vmem(queries.shape, bf16),
            vmem(block, bf16), vmem(block, bf16), vmem(block, bf16),
            vmem((2, TILE, DIM), bf16),
            vmem((3, 3, TILE, DIM), bf16),
            vmem((3, 3, TILE, DIM), bf16),
            vmem((2, 2, 4, HALF, DIM), bf16),
            vmem((2, TILE, DIM), bf16),
            vmem(block, bf16),
            vmem((3, TILE, 2 * TILE), f32),
            vmem((3, TILE, 3 * TILE), f32),
            vmem((2, TILE, DIM), f32),
            vmem((2, TILE, DIM), f32),
            vmem((2, TILE, DIM), f32),
            dma((3,)), dma((3,)), dma((3,)), dma((2,)), dma((2, 4)), dma((2,)), dma((2, 2, 4)),
            dma((2, 2)), dma((2, 2, 4)), dma((2, 4, 3)), dma((2, 2, 4)), dma((2, 2, 4)),
            dma((2, SOURCES)), dma,
        ],
        compiler_params=pltpu.CompilerParams(
            collective_id=0, has_side_effects=True, vmem_limit_bytes=48 * 1024 * 1024
        ),
        cost_estimate=pl.CostEstimate(
            flops=1100000000, bytes_accessed=800000, transcendentals=2200000
        ),
    )(*(pltpu.with_memory_space_constraint(operand, pltpu.HBM) for operand in operands))


def solution(mesh):
    return jax.shard_map(
        per_device,
        mesh=mesh,
        in_specs=(
            P("ta", "ha", "wa", None),
            P("ta", "ha", "wa", None),
            P("ta", "ha", "wa", None),
            P(),
            P(),
        ),
        out_specs=P("ta", "ha", "wa", None),
        check_vma=False,
    )
```

```python
import functools
import math

import jax
import jax.numpy as jnp
from jax import lax
from jax.experimental import pallas as pl
from jax.experimental.pallas import tpu as pltpu
from jax.sharding import PartitionSpec as P

MESH = pl.DeviceIdType.MESH
EPSILON = 1e-06
HEADS = 16
DIM = 128
TOKENS = 48
SOURCES = 8
TILE = SOURCES * TOKENS
HALF = TILE // 2
LINE = 4
SCORE_SCALE = 1.0 / math.sqrt(DIM)
NOTHING = -1e30

ROUTE = ((3, 3, 0, 0), (3, 3, 0, 0))
AWAY = tuple(sorted({away for turns in ROUTE for away in turns if away > 0}))

ARRIVALS = ((0, 1, 2, 3), (1, 0, 2, 3), (2, 1, 3, 0), (3, 2, 1, 0), (3, 2, 1, 0), (3, 2, 0, 1), (0, 3, 1, 2), (0, 1, 2, 3))
PACKED = tuple(sum(order[turn] * 4**place for place, order in enumerate(ARRIVALS)) for turn in range(4))
POWERS = tuple(4**place for place in range(8))


def normed(x, gain):
    mean_sq = jnp.mean(x * x, axis=-1, keepdims=True)
    return x * lax.rsqrt(mean_sq + EPSILON) * gain


def landed(ref, sem):
    pltpu.make_async_copy(ref, ref, sem).wait()


def kernel(
    q_hbm, k_hbm, v_hbm, qg_hbm, kg_hbm, o_ref,
    q_in, k_in, v_in, qg_ref, kg_ref, qs, ks, vs, qb, kb, vb, rb, osend, ob,
    s_narrow, s_wide, m_ref, l_ref, acc_ref,
    in_sem, own_send, own_self, q_recv, own_recv, edge_recv, near_recv, cross_recv, relay_recv,
    fwd_send, relay_send, cross_send, out_send, out_recv, near_ready, up_ready, down_ready,
):
    ta, zl, y = lax.axis_index("ta"), lax.axis_index("ha"), lax.axis_index("wa")
    frame, core = ta // 2, lax.rem(ta, 2)
    other = 1 - core
    x = lax.rem(frame, LINE)
    last_frame = lax.axis_size("ta") // 2 - 1
    chip = y * 2 + zl
    to_core = y // 4
    own = core == to_core
    not_own = jnp.logical_not(own)
    has_low, has_high = frame > 0, frame < last_frame
    has = (has_low, has_high)
    first = frame - x
    turn_low = jnp.logical_and(x == 0, has_low)
    turn_high = jnp.logical_and(x == LINE - 1, has_high)
    relay_up, relay_down = (
        jnp.logical_and(functools.reduce(jnp.logical_or, [x == at for at in places]), exists)
        for places, exists in (
            ([LINE - 1 - away for away in AWAY], first + LINE <= last_frame),
            (AWAY, first > 0),
        )
    )

    def device(f, c, z, w):
        return {"ta": f * 2 + c, "ha": z, "wa": w}

    copies_in = [
        pltpu.make_async_copy(src, dst, in_sem.at[i])
        for i, (src, dst) in enumerate(
            ((k_hbm, k_in), (kg_hbm, kg_ref), (q_hbm, q_in), (qg_hbm, qg_ref), (v_hbm, v_in))
        )
    ]
    for copy in copies_in:
        copy.start()

    barrier = pltpu.get_barrier_semaphore()

    def greet(f, c, z, w):
        pl.semaphore_signal(barrier, inc=1, device_id=device(f, c, z, w), device_id_type=MESH)

    def greet_step(n, carry):
        z, c, w = lax.rem(n // 2, 2), lax.rem(n, 2), core * 4 + n // 4

        @pl.when(jnp.logical_or(w * 2 + z != chip, c != core))
        def _():
            greet(frame, c, z, w)

        return carry

    with jax.named_scope("greet"):
        lax.fori_loop(0, HEADS, greet_step, 0)
    greet(frame, other, zl, y)
    for cond, f in (
        (has_high, frame + 1),
        (relay_up, first + LINE - 1),
        (relay_up, first + LINE),
        *((turn_low, frame + away) for away in AWAY),
        *((turn_high, frame + 1 + away) for away in AWAY),
    ):
        @pl.when(cond)
        def _(f=f):
            greet(f, core, zl, y)

    def count(cond, amount=1):
        return jnp.where(cond, amount, 0)

    greetings = (
        1 + HEADS - count(own) + count(has_low)
        + count(turn_high, len(AWAY)) + count(turn_low, len(AWAY)) + count(relay_down, 2)
    )

    def answer(cond, sem, f):
        @pl.when(cond)
        def _():
            pl.semaphore_signal(sem, inc=1, device_id=device(f, core, zl, y), device_id_type=MESH)

    def answers():
        answer(has_low, near_ready, frame - 1)
        for i, away in enumerate(AWAY):
            answer(turn_low, up_ready, frame - 1 - away)
            answer(jnp.logical_and(relay_down, x == away), down_ready.at[i], first)

    def ready(cond, sem):
        @pl.when(cond)
        def _():
            pl.semaphore_wait(sem, 1)

    col = y // 2
    tile = lax.rem(col, 2)
    rows = pl.ds((lax.rem(y, 2) * 4 + zl * 2 + core) * TOKENS, TOKENS)
    group = lax.rem(y, 4)
    blocks = (
        (0, ks, kb.at[1, col - to_core, rows], own_recv.at[0, group]),
        (1, vs, vb.at[1, col - to_core, rows], own_recv.at[1, group]),
        (2, qs, qb.at[tile, rows], q_recv.at[tile]),
    )

    def block_self(which, source, target, recv):
        return (
            pltpu.make_async_copy(source.at[chip], target, recv),
            pltpu.make_async_remote_copy(
                src_ref=source.at[chip], dst_ref=target,
                send_sem=own_self.at[which], recv_sem=recv,
                device_id=device(frame, other, zl, y), device_id_type=MESH,
            ),
        )

    def send_blocks(block, begin=0, end=HEADS):
        which, source, target, recv = block
        here, there = block_self(which, source, target, recv)

        if begin == 0:
            @pl.when(own)
            def _():
                here.start()

            @pl.when(not_own)
            def _():
                there.start()

        def send_step(j, carry):
            turn = j // 2
            offset = (turn + 1) // 2 * (2 * lax.rem(turn, 2) - 1)
            to_y = lax.rem(y + offset + 8, 8)
            to_z = lax.rem(zl + j, 2)
            pltpu.make_async_remote_copy(
                src_ref=source.at[to_y * 2 + to_z], dst_ref=target,
                send_sem=own_send.at[which], recv_sem=recv,
                device_id=device(frame, to_core, to_z, to_y), device_id_type=MESH,
            ).start()
            return carry

        lax.fori_loop(max(begin, 1), end, send_step, 0)

    def head(ref, n):
        return ref[:, :, :, n * DIM : (n + 1) * DIM].astype(jnp.float32).reshape(TOKENS, DIM)

    with jax.named_scope("norm_keys"):
        copies_in[0].wait()
        copies_in[1].wait()
        for n in range(HEADS):
            ks[n] = normed(head(k_in, n), kg_ref[...]).astype(jnp.bfloat16)
    with jax.named_scope("barrier"):
        pl.semaphore_wait(barrier, greetings)
    with jax.named_scope("sends"):
        send_blocks(blocks[0])
        answers()
        copies_in[4].wait()
        for n in range(HEADS):
            vs[n] = head(v_in, n).astype(jnp.bfloat16)
        send_blocks(blocks[1])
        copies_in[2].wait()
        copies_in[3].wait()
        for n in range(HEADS):
            qs[n] = normed(head(q_in, n), qg_ref[...]).astype(jnp.bfloat16)

    place = lax.rem(y - 4 * core + 8, 8)
    power = jnp.int32(POWERS[0])
    for i in range(1, 8):
        power = jnp.where(place == i, POWERS[i], power)
    bufs = (kb, vb)

    def arriving(turn):
        g = lax.rem(PACKED[turn] // power, 4)
        return g, core + g // 2, pl.ds(lax.rem(g, 2) * HALF, HALF), g // 2 == other

    def forwards(kind, turn):
        buf = bufs[kind]
        g, slot, part, at_edge = arriving(turn)
        copies = []

        def add(i, cond, target, recv, f, c):
            copies.append((cond, pltpu.make_async_remote_copy(
                src_ref=buf.at[1, slot, part], dst_ref=target,
                send_sem=fwd_send.at[kind, turn, i], recv_sem=recv,
                device_id=device(f, c, zl, y), device_id_type=MESH,
            )))

        high = (1, buf.at[0, slot, part], near_recv.at[kind, 0, g], frame + 1, core)
        low = (0, buf.at[2, slot, part], near_recv.at[kind, 1, g], frame - 1, core)
        away = ROUTE[kind][turn]
        if away > 0:
            add(1, turn_high, rb.at[0, kind, turn], relay_recv.at[0, kind, turn], frame - away, core)
            add(0, turn_low, rb.at[1, kind, turn], relay_recv.at[1, kind, turn], frame + away, core)
            add(high[0], jnp.logical_and(has_high, x != LINE - 1), *high[1:])
            add(low[0], jnp.logical_and(has_low, x != 0), *low[1:])
        else:
            add(high[0], has_high, *high[1:])
            add(low[0], has_low, *low[1:])
        add(2, at_edge, buf.at[1, 2 * core, part], edge_recv.at[kind], frame, other)
        return copies

    def answered():
        ready(has_high, near_ready)
        for i in range(len(AWAY)):
            ready(turn_low, down_ready.at[i])

    def each(copies, act):
        for cond, copy in copies:
            @pl.when(cond)
            def _(copy=copy):
                act(copy)

    def pass_on(kind, turns):
        for turn in turns:
            g, slot, part, _ = arriving(turn)
            landed(bufs[kind].at[1, slot, part], own_recv.at[kind, g])
            copies = forwards(kind, turn)
            if (kind, turn) == (0, 0):
                each(copies[-2:], lambda copy: copy.start())
                answered()
                copies = copies[:-2]
            each(copies, lambda copy: copy.start())

    def relay_copy(way, kind, turn):
        g, slot, part, _ = arriving(turn)
        return pltpu.make_async_remote_copy(
            src_ref=rb.at[way, kind, turn], dst_ref=bufs[kind].at[2 * way, slot, part],
            send_sem=relay_send.at[way, kind, turn], recv_sem=near_recv.at[kind, way, g],
            device_id=device(first - 1 if way else first + LINE, core, zl, y), device_id_type=MESH,
        )

    def relays(kind, turns, act):
        for turn in turns:
            away = ROUTE[kind][turn]
            if away > 0:
                for way, cond in (
                    (0, jnp.logical_and(relay_up, x == LINE - 1 - away)),
                    (1, jnp.logical_and(relay_down, x == away)),
                ):
                    @pl.when(cond)
                    def _(way=way):
                        act(way, kind, turn)

    def relay(kind, turns):
        def pass_relay(way, kind, turn):
            landed(rb.at[way, kind, turn], relay_recv.at[way, kind, turn])
            relay_copy(way, kind, turn).start()

        relays(kind, turns, pass_relay)

    first_side = count(x == 0)

    def side(turn):
        i = first_side if turn == 0 else 1 - first_side
        return i, jnp.logical_or(jnp.logical_and(i == 0, has_low), jnp.logical_and(i == 1, has_high))

    def cross_copy(kind, i, turn):
        g, slot, part, at_edge = arriving(turn)
        return at_edge, pltpu.make_async_remote_copy(
            src_ref=bufs[kind].at[2 * i, slot, part], dst_ref=bufs[kind].at[2 * i, 2 * core, part],
            send_sem=cross_send.at[kind, i, g], recv_sem=cross_recv.at[kind, i],
            device_id=device(frame, other, zl, y), device_id_type=MESH,
        )

    def near(kind, i):
        for turn in range(4):
            g, slot, part, _ = arriving(turn)
            landed(bufs[kind].at[2 * i, slot, part], near_recv.at[kind, i, g])
            each([cross_copy(kind, i, turn)], lambda copy: copy.start())

    def crossed(kind, i):
        landed(bufs[kind].at[2 * i, 2 * other], cross_recv.at[kind, i])

    def sides(turn, act):
        i, cond = side(turn)

        @pl.when(cond)
        def _():
            act(i)

    def window(buf, which, p):
        start = core if which == 0 else 0
        return buf[p, pl.ds(start, 2 + which)].reshape((2 + which) * TILE, DIM)

    def score(which, p, fresh=False):
        t, scores = ((core, s_narrow), (other, s_wide))[which]
        s = lax.dot_general(
            qb[t], window(kb, which, p), (((1,), (1,)), ((), ())), preferred_element_type=jnp.float32
        ) * SCORE_SCALE
        scores[p] = s
        best = s[:, :DIM] if fresh else jnp.maximum(m_ref[which], s[:, :DIM])
        for c in range(1, (2 + which) * TILE // DIM):
            best = jnp.maximum(best, s[:, c * DIM : (c + 1) * DIM])
        m_ref[which] = best

    def attend(which, ps, rows, total=None, acc=None):
        scores = (s_narrow, s_wide)[which]
        start = core if which == 0 else 0
        best = m_ref[which, rows]
        for p in ps:
            for c in range(2 + which):
                parts = []
                for d in range(TILE // DIM):
                    lanes = slice(c * TILE + d * DIM, c * TILE + (d + 1) * DIM)
                    w = jnp.exp(scores[p, rows, lanes] - best)
                    total = w if total is None else total + w
                    parts.append(w.astype(jnp.bfloat16))
                part = jnp.dot(
                    jnp.concatenate(parts, axis=1), vb[p, start + c], preferred_element_type=jnp.float32
                )
                acc = part if acc is None else acc + part
        return total, acc

    def out_copy(which, i):
        t = (core, other)[which]
        w, z, c = core * 4 + t * 2 + i // 4, lax.rem(i // 2, 2), lax.rem(i, 2)
        part = osend.at[which, pl.ds(i * TOKENS, TOKENS)]
        here = jnp.logical_and(w * 2 + z == chip, c == core)
        return here, pltpu.make_async_copy(part, ob.at[chip], out_recv), pltpu.make_async_remote_copy(
            src_ref=part, dst_ref=ob.at[chip], send_sem=out_send.at[which, i], recv_sem=out_recv,
            device_id=device(frame, c, z, w), device_id_type=MESH,
        )

    def finish(which, rows, total, acc):
        osend[which, rows] = (acc / jnp.sum(total, axis=1, keepdims=True)).astype(jnp.bfloat16)

    def send_out(which, begin, end):
        def step(i, carry):
            here, local, remote = out_copy(which, i)

            @pl.when(here)
            def _():
                local.start()

            @pl.when(jnp.logical_not(here))
            def _():
                remote.start()

            return carry

        lax.fori_loop(begin, end, step, 0)

    @pl.when(jnp.logical_not(jnp.logical_and(has_low, has_high)))
    def _():
        absent = 2 * (1 - first_side)
        s_narrow[absent] = jnp.full((TILE, 2 * TILE), NOTHING, jnp.float32)
        s_wide[absent] = jnp.full((TILE, 3 * TILE), NOTHING, jnp.float32)
        vb[absent] = jnp.zeros((3, TILE, DIM), jnp.bfloat16)

    for kind in range(2):
        for turn in range(4):
            with jax.named_scope(f"own_blocks_{kind}_{turn}"):
                pass_on(kind, [turn])
                if kind == 0:
                    send_blocks(blocks[2], turn * 4, turn * 4 + 4)
            if kind == 1:
                with jax.named_scope(f"relay_{turn}"):
                    if turn == 0:
                        ready(relay_up, up_ready)
                    if turn < 2:
                        relay(0, [turn])
                    if turn == 3:
                        relay(1, range(2))

    turned = jnp.logical_or(turn_low, turn_high)
    straight = jnp.logical_not(turned)

    def near_last(cond, kind):
        @pl.when(cond)
        def _():
            sides(1, lambda i: near(kind, i))

    with jax.named_scope("near_keys_first"):
        sides(0, lambda i: near(0, i))
    with jax.named_scope("near_keys_straight"):
        near_last(straight, 0)
    with jax.named_scope("queries"):
        landed(qb.at[0], q_recv.at[0])
        landed(qb.at[1], q_recv.at[1])
        landed(kb.at[1, 2 * other], edge_recv.at[0])
    with jax.named_scope("score"):
        score(0, 1, fresh=True)
        score(1, 1, fresh=True)

    def score_side(i):
        score(0, 2 * i)
        crossed(0, i)
        score(1, 2 * i)

    with jax.named_scope("score_first_side"):
        sides(0, score_side)
    with jax.named_scope("near_keys_turned"):
        @pl.when(turned)
        def _():
            sides(1, lambda i: near(0, i))
    with jax.named_scope("near_values_first"):
        sides(0, lambda i: near(1, i))
    with jax.named_scope("near_values_firstlues_straight"):
        near_last(straight, 1)
    with jax.named_scope("score_last_side"):
        sides(1, score_side)
    with jax.named_scope("max"):
        landed(vb.at[1, 2 * other], edge_recv.at[1])
        for which in range(2):
            m_ref[which] = jnp.broadcast_to(jnp.max(m_ref[which], axis=1, keepdims=True), (TILE, DIM))

    halves = (slice(0, HALF), slice(HALF, TILE))
    last_p = 2 * (1 - first_side)

    with jax.named_scope("attend_straight"):
        @pl.when(straight)
        def _():
            for turn in range(2):
                sides(turn, lambda i: crossed(1, i))
            ps = (1, 2 * first_side, last_p)
            for rows in halves:
                finish(0, rows, *attend(0, ps, rows))
            send_out(0, 0, SOURCES)
            for half in range(2):
                finish(1, halves[half], *attend(1, ps, halves[half]))
                send_out(1, 4 * half, 4 * half + 4)

    with jax.named_scope("attend_turned"):
        @pl.when(turned)
        def _():
            sides(0, lambda i: crossed(1, i))
            for which in range(2):
                for rows in halves:
                    l_ref[which, rows], acc_ref[which, rows] = attend(which, (1, 2 * first_side), rows)
            with jax.named_scope("near_values_firstlues_turned"):
                sides(1, lambda i: near(1, i))
            def last(which, rows):
                finish(which, rows, *attend(which, (last_p,), rows, l_ref[which, rows], acc_ref[which, rows]))

            for rows in halves:
                last(0, rows)
            send_out(0, 0, SOURCES)
            sides(1, lambda i: crossed(1, i))
            for half in range(2):
                last(1, halves[half])
                send_out(1, 4 * half, 4 * half + 4)

    with jax.named_scope("sends_left"):
        for which, source, target, recv in blocks:
            many = source.at[pl.ds(0, HEADS - 1)]
            landed(many, own_send.at[which])
            _, there = block_self(which, source, target, recv)

            @pl.when(not_own)
            def _(there=there):
                there.wait_send()

        for kind in range(2):
            for turn in range(4):
                each(forwards(kind, turn), lambda copy: copy.wait_send())
                for i in range(2):
                    at_edge, copy = cross_copy(kind, i, turn)

                    @pl.when(jnp.logical_and(at_edge, has[i]))
                    def _(copy=copy):
                        copy.wait_send()

            relays(kind, range(4), lambda way, kind, turn: relay_copy(way, kind, turn).wait_send())

    with jax.named_scope("outputs_left"):
        def out_done(i, carry):
            for which in range(2):
                here, _, remote = out_copy(which, i)

                @pl.when(jnp.logical_not(here))
                def _(remote=remote):
                    remote.wait_send()

            return carry

        lax.fori_loop(0, SOURCES, out_done, 0)

    with jax.named_scope("outputs_land"):
        landed(ob, out_recv)
    with jax.named_scope("write_out"):
        for n in range(HEADS):
            o = ob[n].astype(jnp.float32).reshape(3, 4, 4, DIM)
            o_ref[:, :, :, n * DIM : (n + 1) * DIM] = o.astype(jnp.bfloat16)


def per_device(queries, keys, values, query_gain, key_gain):
    bf16, f32 = jnp.bfloat16, jnp.float32
    dma, regular, vmem = pltpu.SemaphoreType.DMA, pltpu.SemaphoreType.REGULAR, pltpu.VMEM
    hbm = pl.BlockSpec(memory_space=pl.ANY)
    operands = (queries, keys, values, query_gain.reshape(1, DIM), key_gain.reshape(1, DIM))
    block = (HEADS, TOKENS, DIM)
    return pl.pallas_call(
        kernel,
        out_shape=jax.ShapeDtypeStruct(queries.shape, bf16),
        in_specs=[hbm] * 5,
        out_specs=pl.BlockSpec(memory_space=pltpu.VMEM),
        scratch_shapes=[
            vmem(queries.shape, bf16), vmem(queries.shape, bf16), vmem(queries.shape, bf16),
            vmem((1, DIM), f32), vmem((1, DIM), f32),
            vmem(block, bf16), vmem(block, bf16), vmem(block, bf16),
            vmem((2, TILE, DIM), bf16),
            vmem((3, 3, TILE, DIM), bf16),
            vmem((3, 3, TILE, DIM), bf16),
            vmem((2, 2, 4, HALF, DIM), bf16),
            vmem((2, TILE, DIM), bf16),
            vmem(block, bf16),
            vmem((3, TILE, 2 * TILE), f32),
            vmem((3, TILE, 3 * TILE), f32),
            vmem((2, TILE, DIM), f32),
            vmem((2, TILE, DIM), f32),
            vmem((2, TILE, DIM), f32),
            dma((5,)), dma((3,)), dma((3,)), dma((2,)), dma((2, 4)), dma((2,)), dma((2, 2, 4)),
            dma((2, 2)), dma((2, 2, 4)), dma((2, 4, 3)), dma((2, 2, 4)), dma((2, 2, 4)),
            dma((2, SOURCES)), dma, regular, regular, regular((len(AWAY),)),
        ],
        compiler_params=pltpu.CompilerParams(
            collective_id=0, has_side_effects=True, vmem_limit_bytes=48 * 1024 * 1024
        ),
        cost_estimate=pl.CostEstimate(
            flops=1100000000, bytes_accessed=800000, transcendentals=2200000
        ),
    )(*(pltpu.with_memory_space_constraint(operand, pltpu.HBM) for operand in operands))


def solution(mesh):
    return jax.shard_map(
        per_device,
        mesh=mesh,
        in_specs=(
            P("ta", "ha", "wa", None),
            P("ta", "ha", "wa", None),
            P("ta", "ha", "wa", None),
            P(),
            P(),
        ),
        out_specs=P("ta", "ha", "wa", None),
        check_vma=False,
    )
```

```python
import functools
import math

import jax
import jax.numpy as jnp
from jax import lax
from jax.experimental import pallas as pl
from jax.experimental.pallas import tpu as pltpu
from jax.sharding import PartitionSpec as P

MESH = pl.DeviceIdType.MESH
EPSILON = 1e-06
HEADS = 16
DIM = 128
TOKENS = 48
SOURCES = 8
TILE = SOURCES * TOKENS
HALF = TILE // 2
LINE = 4
SCORE_SCALE = 1.0 / math.sqrt(DIM)
NOTHING = -1e30

ROUTE = ((3, 3, 1, 0), (3, 3, 0, 0))
AWAY = tuple(sorted({away for turns in ROUTE for away in turns if away > 0}))

RELAYS = {
    (0, 2): ((1, 0, 0),),
    (0, 3): ((1, 0, 1),),
    (1, 1): ((0, 0, 0), (1, 1, 0), (0, 0, 2), (1, 0, 2)),
    (1, 2): ((0, 0, 1),),
    (1, 3): ((1, 1, 1), (0, 1, 0), (0, 1, 1)),
}

ARRIVALS = ((0, 1, 2, 3), (1, 0, 2, 3), (2, 1, 3, 0), (3, 2, 1, 0), (3, 2, 1, 0), (3, 2, 0, 1), (0, 3, 1, 2), (0, 1, 2, 3))
PACKED = tuple(sum(order[turn] * 4**place for place, order in enumerate(ARRIVALS)) for turn in range(4))
POWERS = tuple(4**place for place in range(8))


def normed(x, gain):
    mean_sq = jnp.mean(x * x, axis=-1, keepdims=True)
    return x * lax.rsqrt(mean_sq + EPSILON) * gain


def landed(ref, sem):
    pltpu.make_async_copy(ref, ref, sem).wait()


def kernel(
    q_hbm, k_hbm, v_hbm, qg_hbm, kg_hbm, o_ref,
    q_in, k_in, v_in, qg_ref, kg_ref, qs, ks, vs, qb, kb, vb, rb, osend, ob,
    s_narrow, s_wide, m_ref, l_ref, acc_ref,
    in_sem, own_send, own_self, q_recv, own_recv, edge_recv, near_recv, cross_recv, relay_recv,
    fwd_send, relay_send, cross_send, out_send, out_recv, near_ready, up_ready, down_ready,
):
    ta, zl, y = lax.axis_index("ta"), lax.axis_index("ha"), lax.axis_index("wa")
    frame, core = ta // 2, lax.rem(ta, 2)
    other = 1 - core
    x = lax.rem(frame, LINE)
    last_frame = lax.axis_size("ta") // 2 - 1
    chip = y * 2 + zl
    to_core = y // 4
    own = core == to_core
    not_own = jnp.logical_not(own)
    has_low, has_high = frame > 0, frame < last_frame
    has = (has_low, has_high)
    first = frame - x
    turn_low = jnp.logical_and(x == 0, has_low)
    turn_high = jnp.logical_and(x == LINE - 1, has_high)
    relay_up, relay_down = (
        jnp.logical_and(functools.reduce(jnp.logical_or, [x == at for at in places]), exists)
        for places, exists in (
            ([LINE - 1 - away for away in AWAY], first + LINE <= last_frame),
            (AWAY, first > 0),
        )
    )

    def device(f, c, z, w):
        return {"ta": f * 2 + c, "ha": z, "wa": w}

    copies_in = [
        pltpu.make_async_copy(src, dst, in_sem.at[i])
        for i, (src, dst) in enumerate(
            ((k_hbm, k_in), (kg_hbm, kg_ref), (q_hbm, q_in), (qg_hbm, qg_ref), (v_hbm, v_in))
        )
    ]
    for copy in copies_in:
        copy.start()

    barrier = pltpu.get_barrier_semaphore()

    def greet(f, c, z, w):
        pl.semaphore_signal(barrier, inc=1, device_id=device(f, c, z, w), device_id_type=MESH)

    with jax.named_scope("greet"):
        for away in (2, 1, 3, 0):
            w = core * 4 + lax.rem(y + away, 4)
            for z in (1 - zl, zl):
                for c in (other, core):
                    if away == 0 and z is zl and c is core:
                        @pl.when(not_own)
                        def _(w=w, z=z, c=c):
                            greet(frame, c, z, w)
                    else:
                        greet(frame, c, z, w)

    greet(frame, other, zl, y)
    for cond, f in (
        (has_high, frame + 1),
        (relay_up, first + LINE - 1),
        (relay_up, first + LINE),
        *((turn_low, frame + away) for away in AWAY),
        *((turn_high, frame + 1 + away) for away in AWAY),
    ):
        @pl.when(cond)
        def _(f=f):
            greet(f, core, zl, y)

    def count(cond, amount=1):
        return jnp.where(cond, amount, 0)

    greetings = (
        1 + HEADS - count(own) + count(has_low)
        + count(turn_high, len(AWAY)) + count(turn_low, len(AWAY)) + count(relay_down, 2)
    )

    def answer(cond, sem, f):
        @pl.when(cond)
        def _():
            pl.semaphore_signal(sem, inc=1, device_id=device(f, core, zl, y), device_id_type=MESH)

    def answers():
        answer(has_low, near_ready, frame - 1)
        for i, away in enumerate(AWAY):
            answer(turn_low, up_ready, frame - 1 - away)
            answer(jnp.logical_and(relay_down, x == away), down_ready.at[i], first)

    def ready(cond, sem):
        @pl.when(cond)
        def _():
            pl.semaphore_wait(sem, 1)

    col = y // 2
    tile = lax.rem(col, 2)
    rows = pl.ds((lax.rem(y, 2) * 4 + zl * 2 + core) * TOKENS, TOKENS)
    group = lax.rem(y, 4)
    blocks = (
        (0, ks, kb.at[1, col - to_core, rows], own_recv.at[0, group]),
        (1, vs, vb.at[1, col - to_core, rows], own_recv.at[1, group]),
        (2, qs, qb.at[tile, rows], q_recv.at[tile]),
    )

    def block_self(which, source, target, recv):
        return (
            pltpu.make_async_copy(source.at[chip], target, recv),
            pltpu.make_async_remote_copy(
                src_ref=source.at[chip], dst_ref=target,
                send_sem=own_self.at[which], recv_sem=recv,
                device_id=device(frame, other, zl, y), device_id_type=MESH,
            ),
        )

    def send_blocks(block, begin=0, end=HEADS):
        which, source, target, recv = block
        here, there = block_self(which, source, target, recv)

        if begin == 0:
            @pl.when(own)
            def _():
                here.start()

            @pl.when(not_own)
            def _():
                there.start()

        for j in range(max(begin, 1), end):
            turn = j // 2
            offset = (turn + 1) // 2 * (2 * (turn % 2) - 1)
            to_y, to_z = lax.rem(y + offset + 8, 8), 1 - zl if j % 2 else zl
            pltpu.make_async_remote_copy(
                src_ref=source.at[to_y * 2 + to_z], dst_ref=target,
                send_sem=own_send.at[which], recv_sem=recv,
                device_id=device(frame, to_core, to_z, to_y), device_id_type=MESH,
            ).start()

    def head(ref, n):
        return ref[:, :, :, n * DIM : (n + 1) * DIM].astype(jnp.float32).reshape(TOKENS, DIM)

    with jax.named_scope("norm_keys"):
        copies_in[0].wait()
        copies_in[1].wait()
        for n in range(HEADS):
            ks[n] = normed(head(k_in, n), kg_ref[...]).astype(jnp.bfloat16)
    with jax.named_scope("barrier"):
        pl.semaphore_wait(barrier, greetings)
    with jax.named_scope("sends"):
        send_blocks(blocks[0])
        answers()
        copies_in[4].wait()
        for n in range(HEADS):
            vs[n] = head(v_in, n).astype(jnp.bfloat16)
        send_blocks(blocks[1])
        copies_in[2].wait()
        copies_in[3].wait()
        for n in range(HEADS):
            qs[n] = normed(head(q_in, n), qg_ref[...]).astype(jnp.bfloat16)

    place = lax.rem(y - 4 * core + 8, 8)
    power = jnp.int32(POWERS[0])
    for i in range(1, 8):
        power = jnp.where(place == i, POWERS[i], power)
    bufs = (kb, vb)

    def arriving(turn):
        g = lax.rem(PACKED[turn] // power, 4)
        return g, core + g // 2, pl.ds(lax.rem(g, 2) * HALF, HALF), g // 2 == other

    def forwards(kind, turn):
        buf = bufs[kind]
        g, slot, part, at_edge = arriving(turn)
        copies = []

        def add(i, cond, target, recv, f, c):
            copies.append((cond, pltpu.make_async_remote_copy(
                src_ref=buf.at[1, slot, part], dst_ref=target,
                send_sem=fwd_send.at[kind, turn, i], recv_sem=recv,
                device_id=device(f, c, zl, y), device_id_type=MESH,
            )))

        high = (1, buf.at[0, slot, part], near_recv.at[kind, 0, g], frame + 1, core)
        low = (0, buf.at[2, slot, part], near_recv.at[kind, 1, g], frame - 1, core)
        away = ROUTE[kind][turn]
        if away > 0:
            add(1, turn_high, rb.at[0, kind, turn], relay_recv.at[0, kind, turn], frame - away, core)
            add(0, turn_low, rb.at[1, kind, turn], relay_recv.at[1, kind, turn], frame + away, core)
            add(high[0], jnp.logical_and(has_high, x != LINE - 1), *high[1:])
            add(low[0], jnp.logical_and(has_low, x != 0), *low[1:])
        else:
            add(high[0], has_high, *high[1:])
            add(low[0], has_low, *low[1:])
        add(2, at_edge, buf.at[1, 2 * core, part], edge_recv.at[kind], frame, other)
        return copies

    def answered():
        ready(has_high, near_ready)
        for i in range(len(AWAY)):
            ready(turn_low, down_ready.at[i])

    def each(copies, act):
        for cond, copy in copies:
            @pl.when(cond)
            def _(copy=copy):
                act(copy)

    def pass_on(kind, turns):
        for turn in turns:
            g, slot, part, _ = arriving(turn)
            landed(bufs[kind].at[1, slot, part], own_recv.at[kind, g])
            copies = forwards(kind, turn)
            if (kind, turn) == (0, 0):
                each(copies[-2:], lambda copy: copy.start())
                answered()
                copies = copies[:-2]
            each(copies, lambda copy: copy.start())

    def relay_copy(way, kind, turn):
        g, slot, part, _ = arriving(turn)
        return pltpu.make_async_remote_copy(
            src_ref=rb.at[way, kind, turn], dst_ref=bufs[kind].at[2 * way, slot, part],
            send_sem=relay_send.at[way, kind, turn], recv_sem=near_recv.at[kind, way, g],
            device_id=device(first - 1 if way else first + LINE, core, zl, y), device_id_type=MESH,
        )

    def relays(kind, turns, act, ways=(0, 1)):
        for turn in turns:
            away = ROUTE[kind][turn]
            if away > 0:
                for way, cond in (
                    (0, jnp.logical_and(relay_up, x == LINE - 1 - away)),
                    (1, jnp.logical_and(relay_down, x == away)),
                ):
                    if way in ways:
                        @pl.when(cond)
                        def _(way=way):
                            act(way, kind, turn)

    def relay(kind, turns, ways):
        def pass_relay(way, kind, turn):
            landed(rb.at[way, kind, turn], relay_recv.at[way, kind, turn])
            relay_copy(way, kind, turn).start()

        relays(kind, turns, pass_relay, ways)

    first_side = count(x == 0)

    def side(turn):
        i = first_side if turn == 0 else 1 - first_side
        return i, jnp.logical_or(jnp.logical_and(i == 0, has_low), jnp.logical_and(i == 1, has_high))

    def cross_copy(kind, i, turn):
        g, slot, part, at_edge = arriving(turn)
        return at_edge, pltpu.make_async_remote_copy(
            src_ref=bufs[kind].at[2 * i, slot, part], dst_ref=bufs[kind].at[2 * i, 2 * core, part],
            send_sem=cross_send.at[kind, i, g], recv_sem=cross_recv.at[kind, i],
            device_id=device(frame, other, zl, y), device_id_type=MESH,
        )

    def near(kind, i):
        for turn in range(4):
            g, slot, part, _ = arriving(turn)
            landed(bufs[kind].at[2 * i, slot, part], near_recv.at[kind, i, g])
            each([cross_copy(kind, i, turn)], lambda copy: copy.start())

    def crossed(kind, i):
        landed(bufs[kind].at[2 * i, 2 * other], cross_recv.at[kind, i])

    def sides(turn, act):
        i, cond = side(turn)

        @pl.when(cond)
        def _():
            act(i)

    def window(buf, which, p):
        start = core if which == 0 else 0
        return buf[p, pl.ds(start, 2 + which)].reshape((2 + which) * TILE, DIM)

    def score(which, p, fresh=False):
        t, scores = ((core, s_narrow), (other, s_wide))[which]
        s = lax.dot_general(
            qb[t], window(kb, which, p), (((1,), (1,)), ((), ())), preferred_element_type=jnp.float32
        ) * SCORE_SCALE
        scores[p] = s
        best = s[:, :DIM] if fresh else jnp.maximum(m_ref[which], s[:, :DIM])
        for c in range(1, (2 + which) * TILE // DIM):
            best = jnp.maximum(best, s[:, c * DIM : (c + 1) * DIM])
        m_ref[which] = best

    def attend(which, ps, rows, total=None, acc=None):
        scores = (s_narrow, s_wide)[which]
        start = core if which == 0 else 0
        best = m_ref[which, rows]
        for p in ps:
            for c in range(2 + which):
                parts = []
                for d in range(TILE // DIM):
                    lanes = slice(c * TILE + d * DIM, c * TILE + (d + 1) * DIM)
                    w = jnp.exp(scores[p, rows, lanes] - best)
                    total = w if total is None else total + w
                    parts.append(w.astype(jnp.bfloat16))
                part = jnp.dot(
                    jnp.concatenate(parts, axis=1), vb[p, start + c], preferred_element_type=jnp.float32
                )
                acc = part if acc is None else acc + part
        return total, acc

    def out_copy(which, i):
        t = (core, other)[which]
        w, z, c = core * 4 + t * 2 + i // 4, i // 2 % 2, i % 2
        part = osend.at[which, pl.ds(i * TOKENS, TOKENS)]
        here = jnp.logical_and(w * 2 + z == chip, c == core)
        return here, pltpu.make_async_copy(part, ob.at[chip], out_recv), pltpu.make_async_remote_copy(
            src_ref=part, dst_ref=ob.at[chip], send_sem=out_send.at[which, i], recv_sem=out_recv,
            device_id=device(frame, c, z, w), device_id_type=MESH,
        )

    def finish(which, rows, total, acc):
        osend[which, rows] = (acc / jnp.sum(total, axis=1, keepdims=True)).astype(jnp.bfloat16)

    def send_out(which, begin, end):
        for i in range(begin, end):
            here, local, remote = out_copy(which, i)

            @pl.when(here)
            def _(local=local):
                local.start()

            @pl.when(jnp.logical_not(here))
            def _(remote=remote):
                remote.start()

    @pl.when(jnp.logical_not(jnp.logical_and(has_low, has_high)))
    def _():
        absent = 2 * (1 - first_side)
        s_narrow[absent] = jnp.full((TILE, 2 * TILE), NOTHING, jnp.float32)
        s_wide[absent] = jnp.full((TILE, 3 * TILE), NOTHING, jnp.float32)
        vb[absent] = jnp.zeros((3, TILE, DIM), jnp.bfloat16)

    for kind in range(2):
        for turn in range(4):
            with jax.named_scope(f"own_blocks_{kind}_{turn}"):
                pass_on(kind, [turn])
                if kind == 0:
                    send_blocks(blocks[2], turn * 4, turn * 4 + 4)
            with jax.named_scope(f"relay_{kind}_{turn}"):
                for way, relay_kind, relay_turn in RELAYS.get((kind, turn), ()):
                    if (way, relay_kind, relay_turn) == (0, 0, 0):
                        ready(relay_up, up_ready)
                    relay(relay_kind, [relay_turn], (way,))

    turned = jnp.logical_or(turn_low, turn_high)
    straight = jnp.logical_not(turned)

    def near_last(cond, kind):
        @pl.when(cond)
        def _():
            sides(1, lambda i: near(kind, i))

    with jax.named_scope("first_side_keys"):
        sides(0, lambda i: near(0, i))
    with jax.named_scope("straight_keys"):
        near_last(straight, 0)
    with jax.named_scope("queries"):
        landed(qb.at[0], q_recv.at[0])
        landed(qb.at[1], q_recv.at[1])
        landed(kb.at[1, 2 * other], edge_recv.at[0])
    with jax.named_scope("score"):
        score(0, 1, fresh=True)
        score(1, 1, fresh=True)

    def score_side(i):
        score(0, 2 * i)
        crossed(0, i)
        score(1, 2 * i)

    with jax.named_scope("score_first_side"):
        sides(0, score_side)
    with jax.named_scope("turned_keys"):
        @pl.when(turned)
        def _():
            sides(1, lambda i: near(0, i))
    with jax.named_scope("first_side_values"):
        sides(0, lambda i: near(1, i))
    with jax.named_scope("straight_values"):
        near_last(straight, 1)
    with jax.named_scope("score_last_side"):
        sides(1, score_side)
    with jax.named_scope("max"):
        landed(vb.at[1, 2 * other], edge_recv.at[1])
        for which in range(2):
            m_ref[which] = jnp.broadcast_to(jnp.max(m_ref[which], axis=1, keepdims=True), (TILE, DIM))

    halves = (slice(0, HALF), slice(HALF, TILE))
    last_p = 2 * (1 - first_side)

    def gather(which, rows):
        l_ref[which, rows], acc_ref[which, rows] = attend(which, (1, 2 * first_side), rows)

    def last(which, rows):
        finish(which, rows, *attend(which, (last_p,), rows, l_ref[which, rows], acc_ref[which, rows]))

    with jax.named_scope("attend_first"):
        gather(0, slice(0, TILE))
        sides(0, lambda i: crossed(1, i))
        gather(1, slice(0, TILE))
    with jax.named_scope("turned_values"):
        near_last(turned, 1)
    with jax.named_scope("attend_last"):
        for rows in halves:
            last(0, rows)
        send_out(0, 0, SOURCES)
        sides(1, lambda i: crossed(1, i))
        for half in range(2):
            last(1, halves[half])
            send_out(1, 4 * half, 4 * half + 4)

    with jax.named_scope("sends_left"):
        for which, source, target, recv in blocks:
            many = source.at[pl.ds(0, HEADS - 1)]
            landed(many, own_send.at[which])
            _, there = block_self(which, source, target, recv)

            @pl.when(not_own)
            def _(there=there):
                there.wait_send()

        for kind in range(2):
            for turn in range(4):
                each(forwards(kind, turn), lambda copy: copy.wait_send())
                for i in range(2):
                    at_edge, copy = cross_copy(kind, i, turn)

                    @pl.when(jnp.logical_and(at_edge, has[i]))
                    def _(copy=copy):
                        copy.wait_send()

            relays(kind, range(4), lambda way, kind, turn: relay_copy(way, kind, turn).wait_send())

    with jax.named_scope("outputs_left"):
        for i in range(SOURCES):
            for which in range(2):
                here, _, remote = out_copy(which, i)

                @pl.when(jnp.logical_not(here))
                def _(remote=remote):
                    remote.wait_send()

    with jax.named_scope("outputs_land"):
        landed(ob, out_recv)
    with jax.named_scope("write_out"):
        for n in range(HEADS):
            o = ob[n].astype(jnp.float32).reshape(3, 4, 4, DIM)
            o_ref[:, :, :, n * DIM : (n + 1) * DIM] = o.astype(jnp.bfloat16)


def per_device(queries, keys, values, query_gain, key_gain):
    bf16, f32 = jnp.bfloat16, jnp.float32
    dma, regular, vmem = pltpu.SemaphoreType.DMA, pltpu.SemaphoreType.REGULAR, pltpu.VMEM
    hbm = pl.BlockSpec(memory_space=pl.ANY)
    operands = (queries, keys, values, query_gain.reshape(1, DIM), key_gain.reshape(1, DIM))
    block = (HEADS, TOKENS, DIM)
    return pl.pallas_call(
        kernel,
        out_shape=jax.ShapeDtypeStruct(queries.shape, bf16),
        in_specs=[hbm] * 5,
        out_specs=pl.BlockSpec(memory_space=pltpu.VMEM),
        scratch_shapes=[
            vmem(queries.shape, bf16), vmem(queries.shape, bf16), vmem(queries.shape, bf16),
            vmem((1, DIM), f32), vmem((1, DIM), f32),
            vmem(block, bf16), vmem(block, bf16), vmem(block, bf16),
            vmem((2, TILE, DIM), bf16),
            vmem((3, 3, TILE, DIM), bf16),
            vmem((3, 3, TILE, DIM), bf16),
            vmem((2, 2, 4, HALF, DIM), bf16),
            vmem((2, TILE, DIM), bf16),
            vmem(block, bf16),
            vmem((3, TILE, 2 * TILE), f32),
            vmem((3, TILE, 3 * TILE), f32),
            vmem((2, TILE, DIM), f32),
            vmem((2, TILE, DIM), f32),
            vmem((2, TILE, DIM), f32),
            dma((5,)), dma((3,)), dma((3,)), dma((2,)), dma((2, 4)), dma((2,)), dma((2, 2, 4)),
            dma((2, 2)), dma((2, 2, 4)), dma((2, 4, 3)), dma((2, 2, 4)), dma((2, 2, 4)),
            dma((2, SOURCES)), dma, regular, regular, regular((len(AWAY),)),
        ],
        compiler_params=pltpu.CompilerParams(
            collective_id=0, has_side_effects=True, vmem_limit_bytes=48 * 1024 * 1024
        ),
        cost_estimate=pl.CostEstimate(
            flops=1100000000, bytes_accessed=800000, transcendentals=2200000
        ),
    )(*(pltpu.with_memory_space_constraint(operand, pltpu.HBM) for operand in operands))


def solution(mesh):
    return jax.shard_map(
        per_device,
        mesh=mesh,
        in_specs=(
            P("ta", "ha", "wa", None),
            P("ta", "ha", "wa", None),
            P("ta", "ha", "wa", None),
            P(),
            P(),
        ),
        out_specs=P("ta", "ha", "wa", None),
        check_vma=False,
    )
```

```python
import functools
import math

import jax
import jax.numpy as jnp
from jax import lax
from jax.experimental import pallas as pl
from jax.experimental.pallas import tpu as pltpu
from jax.sharding import PartitionSpec as P

MESH = pl.DeviceIdType.MESH
EPSILON = 1e-06
HEADS = 16
DIM = 128
TOKENS = 48
SOURCES = 8
TILE = SOURCES * TOKENS
HALF = TILE // 2
LINE = 4
SCORE_SCALE = 1.0 / math.sqrt(DIM)
NOTHING = -1e30

ROUTE = ((3, 3, 1, 0), (3, 3, 0, 0))
AWAY = tuple(sorted({away for turns in ROUTE for away in turns if away > 0}))

RELAYS = {
    (0, 2): ((1, 0, 0),),
    (0, 3): ((1, 0, 1),),
    (1, 1): ((0, 0, 0), (1, 1, 0), (0, 0, 2), (1, 0, 2)),
    (1, 2): ((0, 0, 1),),
    (1, 3): ((1, 1, 1), (0, 1, 0), (0, 1, 1)),
}

ARRIVALS = ((0, 1, 2, 3), (1, 0, 2, 3), (2, 1, 3, 0), (3, 2, 1, 0), (3, 2, 1, 0), (3, 2, 0, 1), (0, 3, 1, 2), (0, 1, 2, 3))
PACKED = tuple(sum(order[turn] * 4**place for place, order in enumerate(ARRIVALS)) for turn in range(4))
POWERS = tuple(4**place for place in range(8))


def normed(x, gain):
    mean_sq = jnp.mean(x * x, axis=-1, keepdims=True)
    return x * lax.rsqrt(mean_sq + EPSILON) * gain


def landed(ref, sem):
    pltpu.make_async_copy(ref, ref, sem).wait()


def kernel(
    q_hbm, k_hbm, v_hbm, qg_hbm, kg_hbm, o_ref,
    q_in, k_in, v_in, qg_ref, kg_ref, qs, ks, vs, qb, kb, vb, rb, osend, ob,
    s_narrow, s_wide, m_ref, l_ref, acc_ref,
    in_sem, own_send, own_self, q_recv, own_recv, edge_recv, near_recv, cross_recv, relay_recv,
    fwd_send, relay_send, cross_send, out_send, out_recv, near_ready, up_ready, down_ready,
):
    ta, zl, y = lax.axis_index("ta"), lax.axis_index("ha"), lax.axis_index("wa")
    frame, core = ta // 2, lax.rem(ta, 2)
    other = 1 - core
    x = lax.rem(frame, LINE)
    last_frame = lax.axis_size("ta") // 2 - 1
    chip = y * 2 + zl
    to_core = y // 4
    own = core == to_core
    not_own = jnp.logical_not(own)
    has_low, has_high = frame > 0, frame < last_frame
    has = (has_low, has_high)
    first = frame - x
    at_end = jnp.logical_or(x == 0, x == LINE - 1)
    turn_low = jnp.logical_and(x == 0, has_low)
    turn_high = jnp.logical_and(x == LINE - 1, has_high)
    relay_up, relay_down = (
        jnp.logical_and(functools.reduce(jnp.logical_or, [x == at for at in places]), exists)
        for places, exists in (
            ([LINE - 1 - away for away in AWAY], first + LINE <= last_frame),
            (AWAY, first > 0),
        )
    )

    def device(f, c, z, w):
        return {"ta": f * 2 + c, "ha": z, "wa": w}

    copies_in = [
        pltpu.make_async_copy(src, dst, in_sem.at[i])
        for i, (src, dst) in enumerate(
            ((k_hbm, k_in), (kg_hbm, kg_ref), (q_hbm, q_in), (qg_hbm, qg_ref), (v_hbm, v_in))
        )
    ]
    for copy in copies_in:
        copy.start()

    barrier = pltpu.get_barrier_semaphore()

    def greet(f, c, z, w):
        pl.semaphore_signal(barrier, inc=1, device_id=device(f, c, z, w), device_id_type=MESH)

    with jax.named_scope("greet"):
        for away in (2, 1, 3, 0):
            w = core * 4 + lax.rem(y + away, 4)
            for z in (1 - zl, zl):
                for c in (other, core):
                    if away == 0 and z is zl and c is core:
                        @pl.when(not_own)
                        def _(w=w, z=z, c=c):
                            greet(frame, c, z, w)
                    else:
                        greet(frame, c, z, w)

    greet(frame, other, zl, y)
    for cond, f in (
        (has_high, frame + 1),
        (relay_up, first + LINE - 1),
        (relay_up, first + LINE),
        *((turn_low, frame + away) for away in AWAY),
        *((turn_high, frame + 1 + away) for away in AWAY),
    ):
        @pl.when(cond)
        def _(f=f):
            greet(f, core, zl, y)

    def count(cond, amount=1):
        return jnp.where(cond, amount, 0)

    greetings = (
        1 + HEADS - count(own) + count(has_low)
        + count(turn_high, len(AWAY)) + count(turn_low, len(AWAY)) + count(relay_down, 2)
    )

    def answer(cond, sem, f):
        @pl.when(cond)
        def _():
            pl.semaphore_signal(sem, inc=1, device_id=device(f, core, zl, y), device_id_type=MESH)

    def answers():
        answer(has_low, near_ready, frame - 1)
        for i, away in enumerate(AWAY):
            answer(turn_low, up_ready, frame - 1 - away)
            answer(jnp.logical_and(relay_down, x == away), down_ready.at[i], first)

    def ready(cond, sem):
        @pl.when(cond)
        def _():
            pl.semaphore_wait(sem, 1)

    col = y // 2
    tile = lax.rem(col, 2)
    rows = pl.ds((lax.rem(y, 2) * 4 + zl * 2 + core) * TOKENS, TOKENS)
    group = lax.rem(y, 4)
    blocks = (
        (0, ks, kb.at[1, col - to_core, rows], own_recv.at[0, group]),
        (1, vs, vb.at[1, col - to_core, rows], own_recv.at[1, group]),
        (2, qs, qb.at[tile, rows], q_recv.at[tile]),
    )

    def block_self(which, source, target, recv):
        return (
            pltpu.make_async_copy(source.at[chip], target, recv),
            pltpu.make_async_remote_copy(
                src_ref=source.at[chip], dst_ref=target,
                send_sem=own_self.at[which], recv_sem=recv,
                device_id=device(frame, other, zl, y), device_id_type=MESH,
            ),
        )

    def send_blocks(block, begin=0, end=HEADS):
        which, source, target, recv = block
        here, there = block_self(which, source, target, recv)

        if begin == 0:
            @pl.when(own)
            def _():
                here.start()

            @pl.when(not_own)
            def _():
                there.start()

        for j in range(max(begin, 1), end):
            turn = j // 2
            offset = (turn + 1) // 2 * (2 * (turn % 2) - 1)
            to_y, to_z = lax.rem(y + offset + 8, 8), 1 - zl if j % 2 else zl
            pltpu.make_async_remote_copy(
                src_ref=source.at[to_y * 2 + to_z], dst_ref=target,
                send_sem=own_send.at[which], recv_sem=recv,
                device_id=device(frame, to_core, to_z, to_y), device_id_type=MESH,
            ).start()

    def head(ref, n):
        return ref[:, :, :, n * DIM : (n + 1) * DIM].astype(jnp.float32).reshape(TOKENS, DIM)

    with jax.named_scope("norm_keys"):
        copies_in[0].wait()
        copies_in[1].wait()
        for n in range(HEADS):
            ks[n] = normed(head(k_in, n), kg_ref[...]).astype(jnp.bfloat16)
    with jax.named_scope("barrier"):
        pl.semaphore_wait(barrier, greetings)
    with jax.named_scope("sends"):
        send_blocks(blocks[0])
        answers()
        copies_in[4].wait()
        for n in range(HEADS):
            vs[n] = head(v_in, n).astype(jnp.bfloat16)
        @pl.when(at_end)
        def _():
            send_blocks(blocks[1])

        copies_in[2].wait()
        copies_in[3].wait()
        for n in range(HEADS):
            qs[n] = normed(head(q_in, n), qg_ref[...]).astype(jnp.bfloat16)

    place = lax.rem(y - 4 * core + 8, 8)
    power = jnp.int32(POWERS[0])
    for i in range(1, 8):
        power = jnp.where(place == i, POWERS[i], power)
    bufs = (kb, vb)

    def arriving(turn):
        g = lax.rem(PACKED[turn] // power, 4)
        return g, core + g // 2, pl.ds(lax.rem(g, 2) * HALF, HALF), g // 2 == other

    def forwards(kind, turn):
        buf = bufs[kind]
        g, slot, part, at_edge = arriving(turn)
        copies = []

        def add(i, cond, target, recv, f, c):
            copies.append((cond, pltpu.make_async_remote_copy(
                src_ref=buf.at[1, slot, part], dst_ref=target,
                send_sem=fwd_send.at[kind, turn, i], recv_sem=recv,
                device_id=device(f, c, zl, y), device_id_type=MESH,
            )))

        high = (1, buf.at[0, slot, part], near_recv.at[kind, 0, g], frame + 1, core)
        low = (0, buf.at[2, slot, part], near_recv.at[kind, 1, g], frame - 1, core)
        away = ROUTE[kind][turn]
        if away > 0:
            add(1, turn_high, rb.at[0, kind, turn], relay_recv.at[0, kind, turn], frame - away, core)
            add(0, turn_low, rb.at[1, kind, turn], relay_recv.at[1, kind, turn], frame + away, core)
            add(high[0], jnp.logical_and(has_high, x != LINE - 1), *high[1:])
            add(low[0], jnp.logical_and(has_low, x != 0), *low[1:])
        else:
            add(high[0], has_high, *high[1:])
            add(low[0], has_low, *low[1:])
        add(2, at_edge, buf.at[1, 2 * core, part], edge_recv.at[kind], frame, other)
        return copies

    def answered():
        ready(has_high, near_ready)
        for i in range(len(AWAY)):
            ready(turn_low, down_ready.at[i])

    def each(copies, act):
        for cond, copy in copies:
            @pl.when(cond)
            def _(copy=copy):
                act(copy)

    def pass_on(kind, turns):
        for turn in turns:
            g, slot, part, _ = arriving(turn)
            landed(bufs[kind].at[1, slot, part], own_recv.at[kind, g])
            copies = forwards(kind, turn)
            if (kind, turn) == (0, 0):
                each(copies[-2:], lambda copy: copy.start())
                answered()
                copies = copies[:-2]
            each(copies, lambda copy: copy.start())

    def relay_copy(way, kind, turn):
        g, slot, part, _ = arriving(turn)
        return pltpu.make_async_remote_copy(
            src_ref=rb.at[way, kind, turn], dst_ref=bufs[kind].at[2 * way, slot, part],
            send_sem=relay_send.at[way, kind, turn], recv_sem=near_recv.at[kind, way, g],
            device_id=device(first - 1 if way else first + LINE, core, zl, y), device_id_type=MESH,
        )

    def relays(kind, turns, act, ways=(0, 1)):
        for turn in turns:
            away = ROUTE[kind][turn]
            if away > 0:
                for way, cond in (
                    (0, jnp.logical_and(relay_up, x == LINE - 1 - away)),
                    (1, jnp.logical_and(relay_down, x == away)),
                ):
                    if way in ways:
                        @pl.when(cond)
                        def _(way=way):
                            act(way, kind, turn)

    def relay(kind, turns, ways):
        def pass_relay(way, kind, turn):
            landed(rb.at[way, kind, turn], relay_recv.at[way, kind, turn])
            relay_copy(way, kind, turn).start()

        relays(kind, turns, pass_relay, ways)

    first_side = count(x == 0)

    def side(turn):
        i = first_side if turn == 0 else 1 - first_side
        return i, jnp.logical_or(jnp.logical_and(i == 0, has_low), jnp.logical_and(i == 1, has_high))

    def cross_copy(kind, i, turn):
        g, slot, part, at_edge = arriving(turn)
        return at_edge, pltpu.make_async_remote_copy(
            src_ref=bufs[kind].at[2 * i, slot, part], dst_ref=bufs[kind].at[2 * i, 2 * core, part],
            send_sem=cross_send.at[kind, i, g], recv_sem=cross_recv.at[kind, i],
            device_id=device(frame, other, zl, y), device_id_type=MESH,
        )

    def near(kind, i):
        for turn in range(4):
            g, slot, part, _ = arriving(turn)
            landed(bufs[kind].at[2 * i, slot, part], near_recv.at[kind, i, g])
            each([cross_copy(kind, i, turn)], lambda copy: copy.start())

    def crossed(kind, i):
        landed(bufs[kind].at[2 * i, 2 * other], cross_recv.at[kind, i])

    def sides(turn, act):
        i, cond = side(turn)

        @pl.when(cond)
        def _():
            act(i)

    def window(buf, which, p):
        start = core if which == 0 else 0
        return buf[p, pl.ds(start, 2 + which)].reshape((2 + which) * TILE, DIM)

    def score(which, p, fresh=False):
        t, scores = ((core, s_narrow), (other, s_wide))[which]
        s = lax.dot_general(
            qb[t], window(kb, which, p), (((1,), (1,)), ((), ())), preferred_element_type=jnp.float32
        ) * SCORE_SCALE
        scores[p] = s
        best = s[:, :DIM] if fresh else jnp.maximum(m_ref[which], s[:, :DIM])
        for c in range(1, (2 + which) * TILE // DIM):
            best = jnp.maximum(best, s[:, c * DIM : (c + 1) * DIM])
        m_ref[which] = best

    def attend(which, ps, rows, total=None, acc=None):
        scores = (s_narrow, s_wide)[which]
        start = core if which == 0 else 0
        best = m_ref[which, rows]
        for p in ps:
            for c in range(2 + which):
                parts = []
                for d in range(TILE // DIM):
                    lanes = slice(c * TILE + d * DIM, c * TILE + (d + 1) * DIM)
                    w = jnp.exp(scores[p, rows, lanes] - best)
                    total = w if total is None else total + w
                    parts.append(w.astype(jnp.bfloat16))
                part = jnp.dot(
                    jnp.concatenate(parts, axis=1), vb[p, start + c], preferred_element_type=jnp.float32
                )
                acc = part if acc is None else acc + part
        return total, acc

    def out_copy(which, i):
        t = (core, other)[which]
        w, z, c = core * 4 + t * 2 + i // 4, i // 2 % 2, i % 2
        part = osend.at[which, pl.ds(i * TOKENS, TOKENS)]
        here = jnp.logical_and(w * 2 + z == chip, c == core)
        return here, pltpu.make_async_copy(part, ob.at[chip], out_recv), pltpu.make_async_remote_copy(
            src_ref=part, dst_ref=ob.at[chip], send_sem=out_send.at[which, i], recv_sem=out_recv,
            device_id=device(frame, c, z, w), device_id_type=MESH,
        )

    def finish(which, rows, total, acc):
        osend[which, rows] = (acc / jnp.sum(total, axis=1, keepdims=True)).astype(jnp.bfloat16)

    def send_out(which, begin, end):
        for i in range(begin, end):
            here, local, remote = out_copy(which, i)

            @pl.when(here)
            def _(local=local):
                local.start()

            @pl.when(jnp.logical_not(here))
            def _(remote=remote):
                remote.start()

    @pl.when(jnp.logical_not(jnp.logical_and(has_low, has_high)))
    def _():
        absent = 2 * (1 - first_side)
        s_narrow[absent] = jnp.full((TILE, 2 * TILE), NOTHING, jnp.float32)
        s_wide[absent] = jnp.full((TILE, 3 * TILE), NOTHING, jnp.float32)
        vb[absent] = jnp.zeros((3, TILE, DIM), jnp.bfloat16)

    for kind in range(2):
        for turn in range(4):
            with jax.named_scope(f"own_blocks_{kind}_{turn}"):
                pass_on(kind, [turn])
                if (kind, turn) == (0, 0):
                    @pl.when(jnp.logical_not(at_end))
                    def _():
                        send_blocks(blocks[1])

                if kind == 0:
                    send_blocks(blocks[2], turn * 4, turn * 4 + 4)
            with jax.named_scope(f"relay_{kind}_{turn}"):
                for way, relay_kind, relay_turn in RELAYS.get((kind, turn), ()):
                    if (way, relay_kind, relay_turn) == (0, 0, 0):
                        ready(relay_up, up_ready)
                    relay(relay_kind, [relay_turn], (way,))

    turned = jnp.logical_or(turn_low, turn_high)
    straight = jnp.logical_not(turned)

    def near_last(cond, kind):
        @pl.when(cond)
        def _():
            sides(1, lambda i: near(kind, i))

    with jax.named_scope("first_side_keys"):
        sides(0, lambda i: near(0, i))
    with jax.named_scope("straight_keys"):
        near_last(straight, 0)
    with jax.named_scope("queries"):
        landed(qb.at[0], q_recv.at[0])
        landed(qb.at[1], q_recv.at[1])
        landed(kb.at[1, 2 * other], edge_recv.at[0])
    with jax.named_scope("score"):
        score(0, 1, fresh=True)
        score(1, 1, fresh=True)

    def score_side(i):
        score(0, 2 * i)
        crossed(0, i)
        score(1, 2 * i)

    with jax.named_scope("score_first_side"):
        sides(0, score_side)
    with jax.named_scope("turned_keys"):
        @pl.when(turned)
        def _():
            sides(1, lambda i: near(0, i))
    with jax.named_scope("first_side_values"):
        sides(0, lambda i: near(1, i))
    with jax.named_scope("straight_values"):
        near_last(straight, 1)
    with jax.named_scope("score_last_side"):
        sides(1, score_side)
    with jax.named_scope("max"):
        landed(vb.at[1, 2 * other], edge_recv.at[1])
        for which in range(2):
            m_ref[which] = jnp.broadcast_to(jnp.max(m_ref[which], axis=1, keepdims=True), (TILE, DIM))

    halves = (slice(0, HALF), slice(HALF, TILE))
    last_p = 2 * (1 - first_side)

    def gather(which, rows):
        l_ref[which, rows], acc_ref[which, rows] = attend(which, (1, 2 * first_side), rows)

    def last(which, rows):
        finish(which, rows, *attend(which, (last_p,), rows, l_ref[which, rows], acc_ref[which, rows]))

    with jax.named_scope("attend_first"):
        gather(0, slice(0, TILE))
        sides(0, lambda i: crossed(1, i))
        gather(1, slice(0, TILE))
    with jax.named_scope("turned_values"):
        near_last(turned, 1)
    with jax.named_scope("attend_last"):
        for rows in halves:
            last(0, rows)
        send_out(0, 0, SOURCES)
        sides(1, lambda i: crossed(1, i))
        for half in range(2):
            last(1, halves[half])
            send_out(1, 4 * half, 4 * half + 4)

    with jax.named_scope("sends_left"):
        for which, source, target, recv in blocks:
            many = source.at[pl.ds(0, HEADS - 1)]
            landed(many, own_send.at[which])
            _, there = block_self(which, source, target, recv)

            @pl.when(not_own)
            def _(there=there):
                there.wait_send()

        for kind in range(2):
            for turn in range(4):
                each(forwards(kind, turn), lambda copy: copy.wait_send())
                for i in range(2):
                    at_edge, copy = cross_copy(kind, i, turn)

                    @pl.when(jnp.logical_and(at_edge, has[i]))
                    def _(copy=copy):
                        copy.wait_send()

            relays(kind, range(4), lambda way, kind, turn: relay_copy(way, kind, turn).wait_send())

    with jax.named_scope("outputs_left"):
        for i in range(SOURCES):
            for which in range(2):
                here, _, remote = out_copy(which, i)

                @pl.when(jnp.logical_not(here))
                def _(remote=remote):
                    remote.wait_send()

    with jax.named_scope("outputs_land"):
        landed(ob, out_recv)
    with jax.named_scope("write_out"):
        for n in range(HEADS):
            o = ob[n].astype(jnp.float32).reshape(3, 4, 4, DIM)
            o_ref[:, :, :, n * DIM : (n + 1) * DIM] = o.astype(jnp.bfloat16)


def per_device(queries, keys, values, query_gain, key_gain):
    bf16, f32 = jnp.bfloat16, jnp.float32
    dma, regular, vmem = pltpu.SemaphoreType.DMA, pltpu.SemaphoreType.REGULAR, pltpu.VMEM
    hbm = pl.BlockSpec(memory_space=pl.ANY)
    operands = (queries, keys, values, query_gain.reshape(1, DIM), key_gain.reshape(1, DIM))
    block = (HEADS, TOKENS, DIM)
    return pl.pallas_call(
        kernel,
        out_shape=jax.ShapeDtypeStruct(queries.shape, bf16),
        in_specs=[hbm] * 5,
        out_specs=pl.BlockSpec(memory_space=pltpu.VMEM),
        scratch_shapes=[
            vmem(queries.shape, bf16), vmem(queries.shape, bf16), vmem(queries.shape, bf16),
            vmem((1, DIM), f32), vmem((1, DIM), f32),
            vmem(block, bf16), vmem(block, bf16), vmem(block, bf16),
            vmem((2, TILE, DIM), bf16),
            vmem((3, 3, TILE, DIM), bf16),
            vmem((3, 3, TILE, DIM), bf16),
            vmem((2, 2, 4, HALF, DIM), bf16),
            vmem((2, TILE, DIM), bf16),
            vmem(block, bf16),
            vmem((3, TILE, 2 * TILE), f32),
            vmem((3, TILE, 3 * TILE), f32),
            vmem((2, TILE, DIM), f32),
            vmem((2, TILE, DIM), f32),
            vmem((2, TILE, DIM), f32),
            dma((5,)), dma((3,)), dma((3,)), dma((2,)), dma((2, 4)), dma((2,)), dma((2, 2, 4)),
            dma((2, 2)), dma((2, 2, 4)), dma((2, 4, 3)), dma((2, 2, 4)), dma((2, 2, 4)),
            dma((2, SOURCES)), dma, regular, regular, regular((len(AWAY),)),
        ],
        compiler_params=pltpu.CompilerParams(
            collective_id=0, has_side_effects=True, vmem_limit_bytes=48 * 1024 * 1024
        ),
        cost_estimate=pl.CostEstimate(
            flops=1100000000, bytes_accessed=800000, transcendentals=2200000
        ),
    )(*(pltpu.with_memory_space_constraint(operand, pltpu.HBM) for operand in operands))


def solution(mesh):
    return jax.shard_map(
        per_device,
        mesh=mesh,
        in_specs=(
            P("ta", "ha", "wa", None),
            P("ta", "ha", "wa", None),
            P("ta", "ha", "wa", None),
            P(),
            P(),
        ),
        out_specs=P("ta", "ha", "wa", None),
        check_vma=False,
    )
```

```python
import functools
import math

import jax
import jax.numpy as jnp
from jax import lax
from jax.experimental import pallas as pl
from jax.experimental.pallas import tpu as pltpu
from jax.sharding import PartitionSpec as P

MESH = pl.DeviceIdType.MESH
EPSILON = 1e-06
HEADS = 16
DIM = 128
TOKENS = 48
SOURCES = 8
TILE = SOURCES * TOKENS
HALF = TILE // 2
LINE = 4
SCORE_SCALE = 1.0 / math.sqrt(DIM)
NOTHING = -1e30

ROUTE = ((1, 3, 3, 0), (3, 3, 0, 0))
AWAY = tuple(sorted({away for turns in ROUTE for away in turns if away > 0}))

RELAYS = {
    (0, 3): ((1, 0, 1), (0, 0, 0), (1, 0, 0)),
    (1, 0): ((1, 0, 2),),
    (1, 1): ((0, 0, 1), (1, 1, 0)),
    (1, 2): ((0, 0, 2),),
    (1, 3): ((1, 1, 1), (0, 1, 0), (0, 1, 1)),
}

ARRIVALS = ((0, 1, 2, 3), (1, 0, 2, 3), (2, 1, 3, 0), (3, 2, 1, 0), (3, 2, 1, 0), (3, 2, 0, 1), (0, 3, 1, 2), (0, 1, 2, 3))
PACKED = tuple(sum(order[turn] * 4**place for place, order in enumerate(ARRIVALS)) for turn in range(4))
POWERS = tuple(4**place for place in range(8))


def normed(x, gain):
    mean_sq = jnp.mean(x * x, axis=-1, keepdims=True)
    return x * lax.rsqrt(mean_sq + EPSILON) * gain


def landed(ref, sem):
    pltpu.make_async_copy(ref, ref, sem).wait()


def kernel(
    q_hbm, k_hbm, v_hbm, qg_hbm, kg_hbm, o_ref,
    q_in, k_in, v_in, qg_ref, kg_ref, qs, ks, vs, qb, kb, vb, rb, osend, ob,
    s_narrow, s_wide, m_ref, l_ref, acc_ref,
    in_sem, own_send, own_self, q_recv, own_recv, edge_recv, near_recv, cross_recv, relay_recv,
    fwd_send, relay_send, cross_send, out_send, out_recv, near_ready, up_ready, down_ready,
):
    ta, zl, y = lax.axis_index("ta"), lax.axis_index("ha"), lax.axis_index("wa")
    frame, core = ta // 2, lax.rem(ta, 2)
    other = 1 - core
    x = lax.rem(frame, LINE)
    last_frame = lax.axis_size("ta") // 2 - 1
    chip = y * 2 + zl
    to_core = y // 4
    own = core == to_core
    not_own = jnp.logical_not(own)
    has_low, has_high = frame > 0, frame < last_frame
    has = (has_low, has_high)
    first = frame - x
    turn_low = jnp.logical_and(x == 0, has_low)
    turn_high = jnp.logical_and(x == LINE - 1, has_high)
    relay_up, relay_down = (
        jnp.logical_and(functools.reduce(jnp.logical_or, [x == at for at in places]), exists)
        for places, exists in (
            ([LINE - 1 - away for away in AWAY], first + LINE <= last_frame),
            (AWAY, first > 0),
        )
    )

    def device(f, c, z, w):
        return {"ta": f * 2 + c, "ha": z, "wa": w}

    copies_in = [
        pltpu.make_async_copy(src, dst, in_sem.at[i])
        for i, (src, dst) in enumerate(
            ((k_hbm, k_in), (kg_hbm, kg_ref), (q_hbm, q_in), (qg_hbm, qg_ref), (v_hbm, v_in))
        )
    ]
    for copy in copies_in:
        copy.start()

    barrier = pltpu.get_barrier_semaphore()

    def greet(f, c, z, w):
        pl.semaphore_signal(barrier, inc=1, device_id=device(f, c, z, w), device_id_type=MESH)

    with jax.named_scope("greet"):
        for away in (2, 1, 3, 0):
            w = core * 4 + lax.rem(y + away, 4)
            for z in (1 - zl, zl):
                for c in (other, core):
                    if away == 0 and z is zl and c is core:
                        @pl.when(not_own)
                        def _(w=w, z=z, c=c):
                            greet(frame, c, z, w)
                    else:
                        greet(frame, c, z, w)

    greet(frame, other, zl, y)
    for cond, f in (
        (has_high, frame + 1),
        (relay_up, first + LINE - 1),
        (relay_up, first + LINE),
        *((turn_low, frame + away) for away in AWAY),
        *((turn_high, frame + 1 + away) for away in AWAY),
    ):
        @pl.when(cond)
        def _(f=f):
            greet(f, core, zl, y)

    def count(cond, amount=1):
        return jnp.where(cond, amount, 0)

    greetings = (
        1 + HEADS - count(own) + count(has_low)
        + count(turn_high, len(AWAY)) + count(turn_low, len(AWAY)) + count(relay_down, 2)
    )

    def answer(cond, sem, f):
        @pl.when(cond)
        def _():
            pl.semaphore_signal(sem, inc=1, device_id=device(f, core, zl, y), device_id_type=MESH)

    def answers():
        answer(has_low, near_ready, frame - 1)
        for i, away in enumerate(AWAY):
            answer(turn_low, up_ready, frame - 1 - away)
            answer(jnp.logical_and(relay_down, x == away), down_ready.at[i], first)

    def ready(cond, sem):
        @pl.when(cond)
        def _():
            pl.semaphore_wait(sem, 1)

    col = y // 2
    tile = lax.rem(col, 2)
    rows = pl.ds((lax.rem(y, 2) * 4 + zl * 2 + core) * TOKENS, TOKENS)
    group = lax.rem(y, 4)
    blocks = (
        (0, ks, kb.at[1, col - to_core, rows], own_recv.at[0, group]),
        (1, vs, vb.at[1, col - to_core, rows], own_recv.at[1, group]),
        (2, qs, qb.at[tile, rows], q_recv.at[tile]),
    )

    def block_self(which, source, target, recv):
        return (
            pltpu.make_async_copy(source.at[chip], target, recv),
            pltpu.make_async_remote_copy(
                src_ref=source.at[chip], dst_ref=target,
                send_sem=own_self.at[which], recv_sem=recv,
                device_id=device(frame, other, zl, y), device_id_type=MESH,
            ),
        )

    def send_blocks(block, begin=0, end=HEADS):
        which, source, target, recv = block
        here, there = block_self(which, source, target, recv)

        if begin == 0:
            @pl.when(own)
            def _():
                here.start()

            @pl.when(not_own)
            def _():
                there.start()

        for j in range(max(begin, 1), end):
            turn = j // 2
            offset = (turn + 1) // 2 * (2 * (turn % 2) - 1)
            to_y, to_z = lax.rem(y + offset + 8, 8), 1 - zl if j % 2 else zl
            pltpu.make_async_remote_copy(
                src_ref=source.at[to_y * 2 + to_z], dst_ref=target,
                send_sem=own_send.at[which], recv_sem=recv,
                device_id=device(frame, to_core, to_z, to_y), device_id_type=MESH,
            ).start()

    def head(ref, n):
        return ref[:, :, :, n * DIM : (n + 1) * DIM].astype(jnp.float32).reshape(TOKENS, DIM)

    with jax.named_scope("norm_keys"):
        copies_in[0].wait()
        copies_in[1].wait()
        for n in range(HEADS):
            ks[n] = normed(head(k_in, n), kg_ref[...]).astype(jnp.bfloat16)
    with jax.named_scope("barrier"):
        pl.semaphore_wait(barrier, greetings)
    with jax.named_scope("sends"):
        send_blocks(blocks[0])
        answers()
        copies_in[4].wait()
        for n in range(HEADS):
            vs[n] = head(v_in, n).astype(jnp.bfloat16)
        send_blocks(blocks[1])
        copies_in[2].wait()
        copies_in[3].wait()
        for n in range(HEADS):
            qs[n] = normed(head(q_in, n), qg_ref[...]).astype(jnp.bfloat16)

    place = lax.rem(y - 4 * core + 8, 8)
    power = jnp.int32(POWERS[0])
    for i in range(1, 8):
        power = jnp.where(place == i, POWERS[i], power)
    bufs = (kb, vb)

    def arriving(turn):
        g = lax.rem(PACKED[turn] // power, 4)
        return g, core + g // 2, pl.ds(lax.rem(g, 2) * HALF, HALF), g // 2 == other

    def forwards(kind, turn):
        buf = bufs[kind]
        g, slot, part, at_edge = arriving(turn)
        copies = []

        def add(i, cond, target, recv, f, c):
            copies.append((cond, pltpu.make_async_remote_copy(
                src_ref=buf.at[1, slot, part], dst_ref=target,
                send_sem=fwd_send.at[kind, turn, i], recv_sem=recv,
                device_id=device(f, c, zl, y), device_id_type=MESH,
            )))

        high = (1, buf.at[0, slot, part], near_recv.at[kind, 0, g], frame + 1, core)
        low = (0, buf.at[2, slot, part], near_recv.at[kind, 1, g], frame - 1, core)
        away = ROUTE[kind][turn]
        if away > 0:
            add(1, turn_high, rb.at[0, kind, turn], relay_recv.at[0, kind, turn], frame - away, core)
            add(0, turn_low, rb.at[1, kind, turn], relay_recv.at[1, kind, turn], frame + away, core)
            add(high[0], jnp.logical_and(has_high, x != LINE - 1), *high[1:])
            add(low[0], jnp.logical_and(has_low, x != 0), *low[1:])
        else:
            add(high[0], has_high, *high[1:])
            add(low[0], has_low, *low[1:])
        add(2, at_edge, buf.at[1, 2 * core, part], edge_recv.at[kind], frame, other)
        return copies

    def answered():
        ready(has_high, near_ready)
        for i in range(len(AWAY)):
            ready(turn_low, down_ready.at[i])

    def each(copies, act):
        for cond, copy in copies:
            @pl.when(cond)
            def _(copy=copy):
                act(copy)

    def pass_on(kind, turns):
        for turn in turns:
            g, slot, part, _ = arriving(turn)
            landed(bufs[kind].at[1, slot, part], own_recv.at[kind, g])
            copies = forwards(kind, turn)
            if (kind, turn) == (0, 0):
                each(copies[-2:], lambda copy: copy.start())
                answered()
                copies = copies[:-2]
            each(copies, lambda copy: copy.start())

    def relay_copy(way, kind, turn):
        g, slot, part, _ = arriving(turn)
        return pltpu.make_async_remote_copy(
            src_ref=rb.at[way, kind, turn], dst_ref=bufs[kind].at[2 * way, slot, part],
            send_sem=relay_send.at[way, kind, turn], recv_sem=near_recv.at[kind, way, g],
            device_id=device(first - 1 if way else first + LINE, core, zl, y), device_id_type=MESH,
        )

    def relays(kind, turns, act, ways=(0, 1)):
        for turn in turns:
            away = ROUTE[kind][turn]
            if away > 0:
                for way, cond in (
                    (0, jnp.logical_and(relay_up, x == LINE - 1 - away)),
                    (1, jnp.logical_and(relay_down, x == away)),
                ):
                    if way in ways:
                        @pl.when(cond)
                        def _(way=way):
                            act(way, kind, turn)

    def relay(kind, turns, ways):
        def pass_relay(way, kind, turn):
            landed(rb.at[way, kind, turn], relay_recv.at[way, kind, turn])
            relay_copy(way, kind, turn).start()

        relays(kind, turns, pass_relay, ways)

    first_side = count(x == 0)

    def side(turn):
        i = first_side if turn == 0 else 1 - first_side
        return i, jnp.logical_or(jnp.logical_and(i == 0, has_low), jnp.logical_and(i == 1, has_high))

    def cross_copy(kind, i, turn):
        g, slot, part, at_edge = arriving(turn)
        return at_edge, pltpu.make_async_remote_copy(
            src_ref=bufs[kind].at[2 * i, slot, part], dst_ref=bufs[kind].at[2 * i, 2 * core, part],
            send_sem=cross_send.at[kind, i, g], recv_sem=cross_recv.at[kind, i],
            device_id=device(frame, other, zl, y), device_id_type=MESH,
        )

    def near(kind, i):
        for turn in range(4):
            g, slot, part, _ = arriving(turn)
            landed(bufs[kind].at[2 * i, slot, part], near_recv.at[kind, i, g])
            each([cross_copy(kind, i, turn)], lambda copy: copy.start())

    def crossed(kind, i):
        landed(bufs[kind].at[2 * i, 2 * other], cross_recv.at[kind, i])

    def sides(turn, act):
        i, cond = side(turn)

        @pl.when(cond)
        def _():
            act(i)

    def window(buf, which, p):
        start = core if which == 0 else 0
        return buf[p, pl.ds(start, 2 + which)].reshape((2 + which) * TILE, DIM)

    def score(which, p, fresh=False):
        t, scores = ((core, s_narrow), (other, s_wide))[which]
        s = lax.dot_general(
            qb[t], window(kb, which, p), (((1,), (1,)), ((), ())), preferred_element_type=jnp.float32
        ) * SCORE_SCALE
        scores[p] = s
        best = s[:, :DIM] if fresh else jnp.maximum(m_ref[which], s[:, :DIM])
        for c in range(1, (2 + which) * TILE // DIM):
            best = jnp.maximum(best, s[:, c * DIM : (c + 1) * DIM])
        m_ref[which] = best

    def attend(which, ps, rows, total=None, acc=None):
        scores = (s_narrow, s_wide)[which]
        start = core if which == 0 else 0
        best = m_ref[which, rows]
        for p in ps:
            for c in range(2 + which):
                parts = []
                for d in range(TILE // DIM):
                    lanes = slice(c * TILE + d * DIM, c * TILE + (d + 1) * DIM)
                    w = jnp.exp(scores[p, rows, lanes] - best)
                    total = w if total is None else total + w
                    parts.append(w.astype(jnp.bfloat16))
                part = jnp.dot(
                    jnp.concatenate(parts, axis=1), vb[p, start + c], preferred_element_type=jnp.float32
                )
                acc = part if acc is None else acc + part
        return total, acc

    def out_copy(which, i):
        t = (core, other)[which]
        w, z, c = core * 4 + t * 2 + i // 4, i // 2 % 2, i % 2
        part = osend.at[which, pl.ds(i * TOKENS, TOKENS)]
        here = jnp.logical_and(w * 2 + z == chip, c == core)
        return here, pltpu.make_async_copy(part, ob.at[chip], out_recv), pltpu.make_async_remote_copy(
            src_ref=part, dst_ref=ob.at[chip], send_sem=out_send.at[which, i], recv_sem=out_recv,
            device_id=device(frame, c, z, w), device_id_type=MESH,
        )

    def finish(which, rows, total, acc):
        osend[which, rows] = (acc / jnp.sum(total, axis=1, keepdims=True)).astype(jnp.bfloat16)

    def send_out(which, begin, end):
        for i in range(begin, end):
            here, local, remote = out_copy(which, i)

            @pl.when(here)
            def _(local=local):
                local.start()

            @pl.when(jnp.logical_not(here))
            def _(remote=remote):
                remote.start()

    @pl.when(jnp.logical_not(jnp.logical_and(has_low, has_high)))
    def _():
        absent = 2 * (1 - first_side)
        s_narrow[absent] = jnp.full((TILE, 2 * TILE), NOTHING, jnp.float32)
        s_wide[absent] = jnp.full((TILE, 3 * TILE), NOTHING, jnp.float32)
        vb[absent] = jnp.zeros((3, TILE, DIM), jnp.bfloat16)

    for kind in range(2):
        for turn in range(4):
            with jax.named_scope(f"own_blocks_{kind}_{turn}"):
                pass_on(kind, [turn])
                if kind == 0:
                    send_blocks(blocks[2], turn * 4, turn * 4 + 4)
            with jax.named_scope(f"relay_{kind}_{turn}"):
                for way, relay_kind, relay_turn in RELAYS.get((kind, turn), ()):
                    if (way, relay_kind, relay_turn) == (0, 0, 0):
                        ready(relay_up, up_ready)
                    relay(relay_kind, [relay_turn], (way,))

    turned = jnp.logical_or(turn_low, turn_high)
    straight = jnp.logical_not(turned)

    def near_last(cond, kind):
        @pl.when(cond)
        def _():
            sides(1, lambda i: near(kind, i))

    with jax.named_scope("first_side_keys"):
        sides(0, lambda i: near(0, i))
    with jax.named_scope("straight_keys"):
        near_last(straight, 0)
    with jax.named_scope("queries"):
        landed(qb.at[0], q_recv.at[0])
        landed(qb.at[1], q_recv.at[1])
        landed(kb.at[1, 2 * other], edge_recv.at[0])
    with jax.named_scope("score"):
        score(0, 1, fresh=True)
        score(1, 1, fresh=True)

    def score_side(i):
        score(0, 2 * i)
        crossed(0, i)
        score(1, 2 * i)

    with jax.named_scope("score_first_side"):
        sides(0, score_side)
    with jax.named_scope("turned_keys"):
        @pl.when(turned)
        def _():
            sides(1, lambda i: near(0, i))
    with jax.named_scope("first_side_values"):
        sides(0, lambda i: near(1, i))
    with jax.named_scope("straight_values"):
        near_last(straight, 1)
    with jax.named_scope("score_last_side"):
        sides(1, score_side)
    with jax.named_scope("max"):
        landed(vb.at[1, 2 * other], edge_recv.at[1])
        for which in range(2):
            m_ref[which] = jnp.broadcast_to(jnp.max(m_ref[which], axis=1, keepdims=True), (TILE, DIM))

    halves = (slice(0, HALF), slice(HALF, TILE))
    last_p = 2 * (1 - first_side)

    def gather(which, rows):
        l_ref[which, rows], acc_ref[which, rows] = attend(which, (1, 2 * first_side), rows)

    def last(which, rows):
        finish(which, rows, *attend(which, (last_p,), rows, l_ref[which, rows], acc_ref[which, rows]))

    with jax.named_scope("attend_first"):
        gather(0, slice(0, TILE))
        sides(0, lambda i: crossed(1, i))
        gather(1, slice(0, TILE))
    with jax.named_scope("turned_values"):
        near_last(turned, 1)
    with jax.named_scope("attend_last"):
        for rows in halves:
            last(0, rows)
        send_out(0, 0, SOURCES)
        sides(1, lambda i: crossed(1, i))
        for half in range(2):
            last(1, halves[half])
            send_out(1, 4 * half, 4 * half + 4)

    with jax.named_scope("sends_left"):
        for which, source, target, recv in blocks:
            many = source.at[pl.ds(0, HEADS - 1)]
            landed(many, own_send.at[which])
            _, there = block_self(which, source, target, recv)

            @pl.when(not_own)
            def _(there=there):
                there.wait_send()

        for kind in range(2):
            for turn in range(4):
                each(forwards(kind, turn), lambda copy: copy.wait_send())
                for i in range(2):
                    at_edge, copy = cross_copy(kind, i, turn)

                    @pl.when(jnp.logical_and(at_edge, has[i]))
                    def _(copy=copy):
                        copy.wait_send()

            relays(kind, range(4), lambda way, kind, turn: relay_copy(way, kind, turn).wait_send())

    with jax.named_scope("outputs_left"):
        for i in range(SOURCES):
            for which in range(2):
                here, _, remote = out_copy(which, i)

                @pl.when(jnp.logical_not(here))
                def _(remote=remote):
                    remote.wait_send()

    with jax.named_scope("outputs_land"):
        landed(ob, out_recv)
    with jax.named_scope("write_out"):
        for n in range(HEADS):
            o = ob[n].astype(jnp.float32).reshape(3, 4, 4, DIM)
            o_ref[:, :, :, n * DIM : (n + 1) * DIM] = o.astype(jnp.bfloat16)


def per_device(queries, keys, values, query_gain, key_gain):
    bf16, f32 = jnp.bfloat16, jnp.float32
    dma, regular, vmem = pltpu.SemaphoreType.DMA, pltpu.SemaphoreType.REGULAR, pltpu.VMEM
    hbm = pl.BlockSpec(memory_space=pl.ANY)
    operands = (queries, keys, values, query_gain.reshape(1, DIM), key_gain.reshape(1, DIM))
    block = (HEADS, TOKENS, DIM)
    return pl.pallas_call(
        kernel,
        out_shape=jax.ShapeDtypeStruct(queries.shape, bf16),
        in_specs=[hbm] * 5,
        out_specs=pl.BlockSpec(memory_space=pltpu.VMEM),
        scratch_shapes=[
            vmem(queries.shape, bf16), vmem(queries.shape, bf16), vmem(queries.shape, bf16),
            vmem((1, DIM), f32), vmem((1, DIM), f32),
            vmem(block, bf16), vmem(block, bf16), vmem(block, bf16),
            vmem((2, TILE, DIM), bf16),
            vmem((3, 3, TILE, DIM), bf16),
            vmem((3, 3, TILE, DIM), bf16),
            vmem((2, 2, 4, HALF, DIM), bf16),
            vmem((2, TILE, DIM), bf16),
            vmem(block, bf16),
            vmem((3, TILE, 2 * TILE), f32),
            vmem((3, TILE, 3 * TILE), f32),
            vmem((2, TILE, DIM), f32),
            vmem((2, TILE, DIM), f32),
            vmem((2, TILE, DIM), f32),
            dma((5,)), dma((3,)), dma((3,)), dma((2,)), dma((2, 4)), dma((2,)), dma((2, 2, 4)),
            dma((2, 2)), dma((2, 2, 4)), dma((2, 4, 3)), dma((2, 2, 4)), dma((2, 2, 4)),
            dma((2, SOURCES)), dma, regular, regular, regular((len(AWAY),)),
        ],
        compiler_params=pltpu.CompilerParams(
            collective_id=0, has_side_effects=True, vmem_limit_bytes=48 * 1024 * 1024
        ),
        cost_estimate=pl.CostEstimate(
            flops=1100000000, bytes_accessed=800000, transcendentals=2200000
        ),
    )(*(pltpu.with_memory_space_constraint(operand, pltpu.HBM) for operand in operands))


def solution(mesh):
    return jax.shard_map(
        per_device,
        mesh=mesh,
        in_specs=(
            P("ta", "ha", "wa", None),
            P("ta", "ha", "wa", None),
            P("ta", "ha", "wa", None),
            P(),
            P(),
        ),
        out_specs=P("ta", "ha", "wa", None),
        check_vma=False,
    )
```
